256 devices in a mesh: lon: 16 (over z, x_hi), lat: 16 (over x_lo, y, core).
Axes of the slice: x: 4 (x_hi: 2, x_lo: 2; x = x_hi * 2 + x_lo), y: 4, z: 8, core: 2. Of those that a mesh axis runs over, the one named last changes fastest.
Arguments:
- x_field: bfloat16 [8, 96, 192, 192], P(None, 'lat', 'lon'), may hold values from -6 to 6
- cotangent: bfloat16 [8, 96, 192, 192], P(None, 'lat', 'lon'), may hold values from -6 to 6
- gain: float32 [192], replicated, may hold values from 0.5 to 1.5
- w_qkv: bfloat16 [192, 576], replicated, may hold values from -0.4375 to 0.4375
- w_proj: bfloat16 [192, 192], replicated, may hold values from -0.4375 to 0.4375
- bias_table: float32 [64, 6, 3312], P('lat'), may hold values from -4 to 310
- position_index: int32 [144, 144], replicated, may hold values from 0 to 3311, as said below
- valid_rows: int32 [96], replicated, may hold values from 0 to 1, as said below
Outputs:
- d_field: bfloat16 [8, 96, 192, 192], P(None, 'lat', 'lon')
- d_gain: float32 [192], replicated
- d_wqkv: float32 [192, 576], replicated
- d_wproj: float32 [192, 192], replicated
- d_table: float32 [64, 6, 3312], P('lat')
The draws below stay inside these ranges and needn't reach their ends.
Inputs may be any that keep to these rules, and one draw needn't show every extreme that they name: position_index[q, k] depends only on the levels of q and k, their rows in the window and the difference of their columns; each value is taken. valid_rows is 0 on the first one or two and the last one or two rows and 1 elsewhere.
All inputs are finite; a program needn't handle non-finite values.
Results may differ from the reference program's by a relative error of at most 0.022.
Values may be sent and summed in bfloat16 or wider, within the bound.
No kernel may reach another device: no remote copies, remote signals or barrier semaphores. Data moves between devices by JAX's collectives and lax.ppermute only.
A program may use at most 128 MiB of HBM per device.

```python
from functools import partial
import jax
import jax.numpy as jnp
from jax import lax

C = 192
HEADS = 6
Z = 8
WZ = 2
WH = 6
WW = 12
WIN = 144
POS = 3312
LAT = 96
LON = 192
NTYPES = 64


def draw_bias_table(key, part):
    key = jax.random.fold_in(key, 11)
    shape = (NTYPES, HEADS, POS)
    return jnp.clip(jax.random.normal(key, shape, jnp.float32), -4.0, 4.0)


def draw_position_index(key, part):
    key = jax.random.fold_in(key, 5)
    tokens = jnp.arange(WIN, dtype=jnp.int32)
    level_of = tokens // (WH * WW)
    row_of = tokens // WW % WH
    col_of = tokens % WW
    code = ((level_of[:, None] * WZ + level_of[None, :]) * WH * WH + row_of[:, None] * WH + row_of[None, :]) * (2 * WW - 1)
    code = code + (col_of[:, None] - col_of[None, :] + WW - 1)
    relabel = jax.random.permutation(key, POS).astype(jnp.int32)
    return relabel[code].astype(jnp.int32)


def draw_valid_rows(key, part):
    key = jax.random.fold_in(key, 7)
    ends = jax.random.randint(key, (2,), 1, 3)
    rows = jnp.arange(LAT, dtype=jnp.int32)
    return ((rows >= ends[0]) & (rows < LAT - ends[1])).astype(jnp.int32)


def block_scale(rng, shape, cuts, low, top_value):
    loudness, own = 1.0, jax.random.fold_in(rng, 6)
    for axis_at, blocks in cuts:
        draws = jnp.exp(jax.random.uniform(jax.random.fold_in(own, axis_at), (blocks,), jnp.float32, low / len(cuts), top_value / len(cuts)))
        loudness = loudness * jnp.repeat(draws, shape[axis_at] // blocks).reshape([-1 if axis == axis_at else 1 for axis in range(len(shape))])
    return loudness


def gaussian(key, extent, scale, bound, cuts=(), held_as=jnp.bfloat16):
    drawn = jax.random.normal(key, extent, jnp.float32) * scale
    if len(cuts) > 0:
        drawn = block_scale(key, extent, cuts, -0.22, 0.18) * drawn
    return jnp.clip(drawn, min=-bound, max=bound).astype(held_as)


def setup_inputs(seed: int = 0) -> dict:
    key_list = jax.random.split(jax.random.key(seed), 9)
    x_field = gaussian(key_list[0], (Z, LAT, LON, C), 1.0, 6.0, ((1, 16), (2, 16)))
    cotangent = gaussian(key_list[1], (Z, LAT, LON, C), 1.0, 6.0, ((1, 16), (2, 16)))
    gain = jnp.clip(1.0 + 0.1 * jax.random.normal(key_list[2], (C,), jnp.float32), 0.5, 1.5)
    w_qkv = gaussian(key_list[3], (C, 3 * C), C ** -0.5, 0.4375)
    w_proj = gaussian(key_list[4], (C, C), C ** -0.5, 0.4375)
    bias_table = draw_bias_table(jax.random.fold_in(key_list[8], 71), 0)
    position_index = draw_position_index(jax.random.fold_in(key_list[8], 71), 0)
    valid_rows = draw_valid_rows(jax.random.fold_in(key_list[8], 71), 0)
    return {"x_field": x_field, "cotangent": cotangent, "gain": gain, "w_qkv": w_qkv, "w_proj": w_proj, "bias_table": bias_table, "position_index": position_index, "valid_rows": valid_rows}


def mult(form, left, right):
    return jnp.einsum(form, left.astype(jnp.float32), right.astype(jnp.float32))

def to_windows(field):
    levels, rows, cols, width = field.shape
    shaped = field.reshape(levels // WZ, WZ, rows // WH, WH, cols // WW, WW, width)
    return shaped.transpose(2, 0, 4, 1, 3, 5, 6).reshape(rows // WH, levels // WZ, cols // WW, WIN, width)

def from_windows(blocks):
    row_blocks, level_blocks, col_blocks, count, width = blocks.shape
    shaped = blocks.reshape(row_blocks, level_blocks, col_blocks, WZ, WH, WW, width)
    return shaped.transpose(1, 3, 0, 4, 2, 5, 6).reshape(level_blocks * WZ, row_blocks * WH, col_blocks * WW, width)

def block_grads(carry, inputs, w_qkv, w_proj, gain, position_index, lat_total):
    x_blk, dy_blk, table_blk, valid_win, lat_start = inputs
    level_blocks, col_blocks, count, width = x_blk.shape
    head_dim = width // HEADS
    scale = head_dim ** (-0.5)
    x_float = x_blk.astype(jnp.float32)
    average = lax.optimization_barrier(jnp.mean(x_float, axis=-1, keepdims=True))
    centred = x_float - average
    inv_std = lax.rsqrt(lax.optimization_barrier(jnp.mean(centred * centred, axis=-1, keepdims=True)) + 1e-05)
    normed = centred * inv_std
    hidden = (normed * gain).astype(jnp.bfloat16).reshape(-1, width)
    qkv = jnp.dot(hidden, w_qkv, preferred_element_type=jnp.float32).astype(jnp.bfloat16)
    qkv = qkv.reshape(level_blocks, col_blocks, count, 3, HEADS, head_dim)
    queries = qkv[:, :, :, 0]
    keys_win = qkv[:, :, :, 1]
    values_win = qkv[:, :, :, 2]
    flat_index = position_index.reshape(-1)
    bias = jnp.take(table_blk, flat_index, axis=2).reshape(level_blocks, HEADS, count, count)
    tokens = jnp.arange(count, dtype=jnp.int32)
    level_of = jnp.arange(level_blocks, dtype=jnp.int32)[:, None] * WZ + tokens[None, :] // (WH * WW)
    row_of = tokens // WW % WH
    region = (level_of == Z - 1).astype(jnp.int32) + 2 * (lat_start + row_of >= lat_total - WH // 2).astype(jnp.int32)[None, :]
    key_ok = lax.optimization_barrier(jnp.sum(valid_win[None, :] * (row_of[:, None] == jnp.arange(WH, dtype=jnp.int32)[None, :]).astype(jnp.int32), axis=1))
    allowed = (region[:, :, None] == region[:, None, :]) & (key_ok[None, None, :] > 0)
    scores = mult('zwqhd,zwkhd->zwhqk', queries, keys_win) * scale + bias[:, None]
    scores = jnp.where(allowed[:, None, None], scores, -1e+30)
    row_max = lax.optimization_barrier(jnp.max(scores, axis=-1, keepdims=True))
    raised = jnp.exp(scores - row_max)
    probs = raised / lax.optimization_barrier(jnp.sum(raised, axis=-1, keepdims=True))
    probs_b = probs.astype(jnp.bfloat16)
    attended = mult('zwhqk,zwkhd->zwqhd', probs_b, values_win).astype(jnp.bfloat16).reshape(-1, width)
    grad_rows = dy_blk.reshape(-1, width)
    d_attended = jnp.dot(grad_rows, w_proj.T, preferred_element_type=jnp.float32).astype(jnp.bfloat16)
    d_attended = d_attended.reshape(level_blocks, col_blocks, count, HEADS, head_dim)
    d_wproj = lax.dot_general(attended, grad_rows, (((0,), (0,)), ((), ())), preferred_element_type=jnp.float32)
    d_probs = mult('zwqhd,zwkhd->zwhqk', d_attended, values_win)
    d_scores = probs * (d_probs - lax.optimization_barrier(jnp.sum(d_probs * probs, axis=-1, keepdims=True)))
    d_bias = lax.optimization_barrier(jnp.sum(d_scores, axis=1)).reshape(level_blocks * HEADS, count * count)
    d_table = jax.ops.segment_sum(d_bias.T, flat_index, num_segments=POS).T.reshape(level_blocks, HEADS, POS)
    d_scores_b = (d_scores * scale).astype(jnp.bfloat16)
    d_queries = mult('zwhqk,zwkhd->zwqhd', d_scores_b, keys_win).astype(jnp.bfloat16)
    d_keys = mult('zwhqk,zwqhd->zwkhd', d_scores_b, queries).astype(jnp.bfloat16)
    d_values = mult('zwhqk,zwqhd->zwkhd', probs_b, d_attended).astype(jnp.bfloat16)
    d_qkv = jnp.stack([d_queries, d_keys, d_values], axis=3).reshape(-1, 3 * width)
    d_wqkv = lax.dot_general(hidden, d_qkv, (((0,), (0,)), ((), ())), preferred_element_type=jnp.float32)
    d_hidden = jnp.dot(d_qkv, w_qkv.T, preferred_element_type=jnp.float32).reshape(x_blk.shape)
    d_gain = lax.optimization_barrier(jnp.sum(d_hidden * normed, axis=(0, 1, 2)))
    d_norm = d_hidden * gain
    branch = inv_std * (d_norm - lax.optimization_barrier(jnp.mean(d_norm, axis=-1, keepdims=True)) - normed * lax.optimization_barrier(jnp.mean(d_norm * normed, axis=-1, keepdims=True)))
    carry = (carry[0] + d_wqkv, carry[1] + d_wproj, carry[2] + d_gain)
    return (carry, (branch.astype(jnp.bfloat16), d_table))

def reference(x_field, cotangent, gain, w_qkv, w_proj, bias_table, position_index, valid_rows):
    stacked = jnp.stack([x_field, cotangent])
    stacked = jnp.roll(stacked, (-(WZ // 2), -(WH // 2), -(WW // 2)), axis=(1, 2, 3))
    x_win = to_windows(stacked[0])
    dy_win = to_windows(stacked[1])
    rolled_valid = jnp.roll(valid_rows, -(WH // 2)).reshape(-1, WH)
    starts = WH * jnp.arange(LAT // WH, dtype=jnp.int32)
    table = bias_table.reshape(LAT // WH, Z // WZ, HEADS, POS)
    width = x_field.shape[3]
    initial = (jnp.zeros((width, 3 * width), jnp.float32), jnp.zeros((width, width), jnp.float32), jnp.zeros((width,), jnp.float32))
    step_fn = partial(block_grads, w_qkv=w_qkv, w_proj=w_proj, gain=gain, position_index=position_index, lat_total=LAT)
    totals, (branch, d_table) = lax.scan(step_fn, initial, (x_win, dy_win, table, rolled_valid, starts))
    branch = jnp.roll(from_windows(branch), (WZ // 2, WH // 2, WW // 2), axis=(0, 1, 2))
    d_field = (cotangent.astype(jnp.float32) + branch.astype(jnp.float32)).astype(jnp.bfloat16)
    grad_scale = (Z * LAT * LON) ** (-0.5)
    table_scale = LON ** (-0.5)
    d_table = d_table.reshape(NTYPES, HEADS, POS) * table_scale
    return (d_field, totals[2] * grad_scale, totals[0] * grad_scale, totals[1] * grad_scale, d_table)
```

```python
import functools

import jax
import jax.numpy as jnp
from jax import lax
from jax.experimental import pallas as pl
from jax.experimental.pallas import tpu as pltpu
from jax.sharding import PartitionSpec as P

HEADS = 6
Z = 8
WZ = 2
WH = 6
WW = 12
WIN = 144
POS = 3312
C = 192
HD = 32
TYPES = 4
GROUPS = TYPES * HEADS
PAIRS = 12
SPAN = 2 * WW - 1
LANES = 384
CHUNKS = 26
SCALE = HD**-0.5
NEG = -1e30
WROWS = 1168
TROWS = 640
F32 = jnp.float32
BF16 = jnp.bfloat16


def nn(left, right):
    return lax.dot_general(left, right, (((1,), (0,)), ((), ())), preferred_element_type=F32)


def nt(left, right):
    return lax.dot_general(left, right, (((1,), (1,)), ((), ())), preferred_element_type=F32)


def bias_kernel(table, index, key_marks, query_marks, bias, inverse, codes):
    acc = [[None] * 3 for _ in range(3)]
    for place in range(PAIRS):
        parts = []
        for col in range(3):
            entry = index[place : place + 1, col * 128 : (col + 1) * 128]
            entry = jnp.broadcast_to(entry, (GROUPS, 128))
            high = lax.shift_right_arithmetic(entry, 7)
            low = lax.bitwise_and(entry, 127)
            found = jnp.zeros((GROUPS, 128), F32)
            for chunk in range(CHUNKS):
                source = table[:, chunk * 128 : (chunk + 1) * 128]
                found = jnp.where(
                    high == chunk, jnp.take_along_axis(source, low, axis=1), found
                )
            parts.append(found)
        row = jnp.concatenate(parts, axis=1)
        moved = pltpu.roll(row, 12, 1)
        for col in range(3):
            at = slice(col * 128, (col + 1) * 128)
            codes[col, pl.ds(place, GROUPS, stride=24), :] = row[:, at]
            codes[col, pl.ds(PAIRS + place, GROUPS, stride=24), :] = moved[:, at]
    for window in range(TYPES):
        allowed = (key_marks[:, window : window + 1] == query_marks[window : window + 1, :]) & (
            key_marks[:, TYPES : TYPES + 1] > 0
        )
        for head in range(HEADS):
            group = window * HEADS + head
            block = jnp.concatenate(
                [codes[col, group * 24 : (group + 1) * 24, :] for col in range(3)], axis=1
            )
            pieces = []
            for step in range(WW // 2):
                turned = pltpu.roll(block, LANES - (132 - 24 * step), 1)
                pieces.append(turned[:, :WIN])
            full = jnp.concatenate(pieces, axis=0)
            bias[group] = jnp.where(allowed, full, NEG)
    total = jnp.zeros((96, 128), F32)
    lane = lax.broadcasted_iota(jnp.int32, (32, LANES), 1)
    tall = lax.broadcasted_iota(jnp.int32, (32, LANES), 0)
    deep = lax.broadcasted_iota(jnp.int32, (128, LANES), 0)
    for place in range(PAIRS):
        entry = index[place : place + 1, :]
        high = lax.shift_right_arithmetic(entry, 7)
        low = lax.bitwise_and(entry, 127)
        hit = high == tall
        left = jnp.concatenate(
            [
                jnp.where(hit, float(place), 0.0),
                jnp.where(hit, lax.shift_right_logical(lane, 7).astype(F32), 0.0),
                jnp.where(hit, lax.bitwise_and(lane, 127).astype(F32), 0.0),
            ],
            axis=0,
        ).astype(BF16)
        right = jnp.where(deep == low, 1.0, 0.0).astype(BF16)
        total = total + nt(left, right)
    total = total.astype(jnp.int32)
    inverse[:32, :] = total[:32] * 3 + total[32:64]
    inverse[32:, :] = total[64:]


def window_kernel(
    x, dy, bias, gain, wq, wq_t, wp, branch, codes, weights, dw_total, dp_total, dg_total
):
    step = pl.program_id(0)

    @pl.when(step == 0)
    def _():
        dw_total[...] = jnp.zeros_like(dw_total)
        dp_total[...] = jnp.zeros_like(dp_total)
        dg_total[...] = jnp.zeros_like(dg_total)

    tokens = x[0].astype(F32)
    average = jnp.mean(tokens, axis=1, keepdims=True)
    centred = tokens - average
    inv_std = lax.rsqrt(jnp.mean(centred * centred, axis=1, keepdims=True) + 1e-5)
    normed = centred * inv_std
    gains = gain[...]
    hidden = (normed * gains).astype(BF16)
    grads = dy[0]
    keys = nn(hidden, wq[:, C : 2 * C]).astype(BF16)
    values = nn(hidden, wq[:, 2 * C :]).astype(BF16)
    qkv_t = nt(wq_t[...], hidden).astype(BF16)
    datt_t = nt(wp[...], grads).astype(BF16)

    def padded(rows, head):
        parts = []
        if head > 0:
            parts.append(jnp.zeros((head * HD, WIN), BF16))
        parts.append(rows)
        if head < HEADS - 1:
            parts.append(jnp.zeros(((HEADS - 1 - head) * HD, WIN), BF16))
        return jnp.concatenate(parts, axis=0)

    att, dq, dk, dv = [], [], [], []
    for head in range(HEADS):
        q_t = qkv_t[head * HD : (head + 1) * HD]
        k_t = qkv_t[C + head * HD : C + (head + 1) * HD]
        v_t = qkv_t[2 * C + head * HD : 2 * C + (head + 1) * HD]
        a_t = datt_t[head * HD : (head + 1) * HD]
        scores = nn(keys, padded(q_t, head)) * SCALE + bias[head]
        raised = jnp.exp(scores - jnp.max(scores, axis=0, keepdims=True))
        probs = raised * (1.0 / jnp.sum(raised, axis=0, keepdims=True))
        probs_b = probs.astype(BF16)
        att.append(nn(v_t, probs_b).astype(BF16))
        d_probs = nn(values, padded(a_t, head))
        d_scores = probs * (d_probs - jnp.sum(d_probs * probs, axis=0, keepdims=True))
        d_scores_b = (d_scores * SCALE).astype(BF16)
        dq.append(nn(k_t, d_scores_b).astype(BF16))
        dk.append(nt(q_t, d_scores_b).astype(BF16))
        dv.append(nt(a_t, probs_b).astype(BF16))
        folded = None
        for part in range(WW // 2):
            rows = d_scores[part * 24 : (part + 1) * 24]
            rows = jnp.concatenate([rows, jnp.zeros((24, LANES - WIN), F32)], axis=1)
            folded = rows if part == 0 else pltpu.roll(folded, 24, 1) + rows
        codes[head] = pltpu.roll(folded, 12, 1)
    att_t = jnp.concatenate(att, axis=0)
    dqkv_t = jnp.concatenate(dq + dk + dv, axis=0)
    dp_total[...] += nn(att_t, grads)
    dw_total[...] += nn(dqkv_t, hidden)
    d_hidden = nn(wq[...], dqkv_t).T
    dg_total[...] += jnp.sum(d_hidden * normed, axis=0, keepdims=True)
    d_norm = d_hidden * gains
    branch[0] = (
        inv_std
        * (
            d_norm
            - jnp.mean(d_norm, axis=1, keepdims=True)
            - normed * jnp.mean(d_norm * normed, axis=1, keepdims=True)
        )
    ).astype(BF16)

    @pl.when(step == TYPES - 1)
    def _():
        dw, dp, dg = dw_total[...], dp_total[...], dg_total[...]
        weights[0:576, :] = dw[:, :128].astype(BF16)
        weights[576:864, :] = jnp.concatenate([dw[:288, 128:], dw[288:, 128:]], axis=1).astype(BF16)
        weights[864:1056, :] = dp[:, :128].astype(BF16)
        weights[1056:1152, :] = jnp.concatenate([dp[:96, 128:], dp[96:, 128:]], axis=1).astype(BF16)
        wide = jnp.concatenate([dg, jnp.zeros((1, 64), F32)], axis=1)
        last = jnp.concatenate([wide[:, :128], wide[:, 128:], jnp.zeros((14, 128), F32)], axis=0)
        weights[1152:1168, :] = last.astype(BF16)


def table_kernel(codes, inverse, packed, rows):
    for place in range(PAIRS):
        above = jnp.concatenate(
            [codes[col, pl.ds(place, GROUPS, stride=24), :] for col in range(3)], axis=1
        )
        below = jnp.concatenate(
            [codes[col, pl.ds(PAIRS + place, GROUPS, stride=24), :] for col in range(3)], axis=1
        )
        whole = above + pltpu.roll(below, LANES - 12, 1)
        for col in range(3):
            rows[place * 3 + col] = whole[:, col * 128 : (col + 1) * 128]
    for chunk in range(CHUNKS):
        source = jnp.broadcast_to(inverse[chunk : chunk + 1, :], (GROUPS, 128))
        low = jnp.broadcast_to(inverse[32 + chunk : 33 + chunk, :], (GROUPS, 128))
        found = jnp.zeros((GROUPS, 128), F32)
        for at in range(3 * PAIRS):
            found = jnp.where(source == at, jnp.take_along_axis(rows[at], low, axis=1), found)
        packed[chunk * 24 : (chunk + 1) * 24, :] = found.astype(BF16)
    packed[CHUNKS * 24 :, :] = jnp.zeros((TROWS - CHUNKS * 24, 128), BF16)


def finish_kernel(grad_scale, table_scale, packed_w, packed_t, d_gain, d_wqkv, d_wproj, d_table):
    scaled = packed_w[...].astype(F32) * grad_scale
    side = scaled[576:864]
    right = jnp.concatenate([side[:, :64], side[:, 64:]], axis=0)
    d_wqkv[...] = jnp.concatenate([scaled[:576], right], axis=1).T
    side = scaled[1056:1152]
    right = jnp.concatenate([side[:, :64], side[:, 64:]], axis=0)
    d_wproj[...] = jnp.concatenate([scaled[864:1056], right], axis=1)
    d_gain[...] = jnp.concatenate([scaled[1152:1153], scaled[1153:1154, :64]], axis=1)
    for chunk in range(CHUNKS):
        part = packed_t[chunk * 24 : (chunk + 1) * 24, :].astype(F32) * table_scale
        width = min(128, POS - chunk * 128)
        for window in range(TYPES):
            d_table[window, :, chunk * 128 : chunk * 128 + width] = part[
                window * HEADS : (window + 1) * HEADS, :width
            ]


def place_index(position_index):
    shaped = position_index.reshape(WZ, WH, WW, WZ, WH, WW)
    first = shaped[:, :, 0, :, :, 1:][..., ::-1].transpose(2, 3, 4, 0, 1)
    second = shaped[:, :, :, :, :, 0].transpose(3, 4, 2, 0, 1)
    both = jnp.concatenate([first, second], axis=2).reshape(PAIRS, SPAN * PAIRS)
    return jnp.pad(both, ((0, 0), (0, LANES - SPAN * PAIRS)), constant_values=-1)


def marks(valid_rows, row_base):
    token = jnp.arange(WIN, dtype=jnp.int32)
    level = token // WH % WZ
    row = token % WH
    top = jnp.arange(TYPES, dtype=jnp.int32)[:, None] * WZ + level[None, :] == Z - 1
    late = row_base + row >= valid_rows.shape[0] - WH // 2
    region = top.astype(F32) + 2.0 * late.astype(F32)[None, :]
    rolled = lax.dynamic_slice_in_dim(jnp.roll(valid_rows, -(WH // 2)), row_base, WH)
    good = jnp.tile(rolled, WIN // WH).astype(F32)
    key_marks = jnp.concatenate([region, good[None, :], jnp.zeros((3, WIN), F32)], axis=0).T
    query_marks = jnp.concatenate([region, jnp.zeros((4, WIN), F32)], axis=0)
    return key_marks, query_marks


def shifted(value, steps_lon, steps_lat):
    lons, lats = lax.axis_size("lon"), lax.axis_size("lat")
    pairs = [
        (i * lats + j, (i + steps_lon) % lons * lats + (j + steps_lat) % lats)
        for i in range(lons)
        for j in range(lats)
    ]
    return lax.ppermute(value, ("lon", "lat"), pairs)


def exchange(value, axis):
    return lax.all_to_all(value, axis, 0, 0)


def added(pieces):
    return jnp.sum(pieces.astype(F32), axis=0).astype(BF16)


def spread(piece, axis):
    count = lax.axis_size(axis)
    return exchange(jnp.broadcast_to(piece[None], (count,) + piece.shape), axis)


def whole(shape):
    return pl.BlockSpec(shape, lambda i: (0,) * len(shape))


def per_device(x_field, cotangent, gain, w_qkv, w_proj, bias_table, position_index, valid_rows):
    half_r, half_c = WH // 2, WW // 2
    stacked = jnp.stack([x_field, cotangent])
    east = shifted(stacked[:, :, :, :half_c], -1, 0)
    south = shifted(stacked[:, :, :half_r], 0, -1)
    corner = shifted(stacked[:, :, :half_r, :half_c], -1, -1)

    row_base = lax.axis_index("lat") * WH
    key_marks, query_marks = marks(valid_rows, row_base)
    index = place_index(position_index)
    table = jnp.pad(bias_table.reshape(GROUPS, POS), ((0, 0), (0, CHUNKS * 128 - POS)))
    bias, inverse = pl.pallas_call(
        bias_kernel,
        out_shape=(
            jax.ShapeDtypeStruct((GROUPS, WIN, WIN), F32),
            jax.ShapeDtypeStruct((64, 128), jnp.int32),
        ),
        scratch_shapes=[pltpu.VMEM((3, GROUPS * 24, 128), F32)],
        compiler_params=pltpu.CompilerParams(vmem_limit_bytes=40 * 2**20),
        name="bias_lookup",
    )(table, index, key_marks, query_marks)

    upper = jnp.concatenate([stacked[:, :, half_r:, half_c:], east[:, :, half_r:]], axis=3)
    lower = jnp.concatenate([south[:, :, :, half_c:], corner], axis=3)
    grid = jnp.roll(jnp.concatenate([upper, lower], axis=2), -(WZ // 2), axis=1)
    tokens = grid.reshape(2, TYPES, WZ, WH, WW, C).transpose(0, 1, 4, 2, 3, 5)
    tokens = tokens.reshape(2, TYPES, WIN, C)

    branch, codes, weights = pl.pallas_call(
        window_kernel,
        grid=(TYPES,),
        in_specs=[
            pl.BlockSpec((1, WIN, C), lambda i: (i, 0, 0)),
            pl.BlockSpec((1, WIN, C), lambda i: (i, 0, 0)),
            pl.BlockSpec((HEADS, WIN, WIN), lambda i: (i, 0, 0)),
            whole((1, C)),
            whole((C, 3 * C)),
            whole((3 * C, C)),
            whole((C, C)),
        ],
        out_specs=(
            pl.BlockSpec((1, WIN, C), lambda i: (i, 0, 0)),
            pl.BlockSpec((HEADS, 24, LANES), lambda i: (i, 0, 0)),
            whole((WROWS, 128)),
        ),
        out_shape=(
            jax.ShapeDtypeStruct((TYPES, WIN, C), BF16),
            jax.ShapeDtypeStruct((GROUPS, 24, LANES), F32),
            jax.ShapeDtypeStruct((WROWS, 128), BF16),
        ),
        scratch_shapes=[
            pltpu.VMEM((3 * C, C), F32),
            pltpu.VMEM((C, C), F32),
            pltpu.VMEM((1, C), F32),
        ],
        compiler_params=pltpu.CompilerParams(vmem_limit_bytes=40 * 2**20),
        name="window_grads",
    )(tokens[0], tokens[1], bias, gain.reshape(1, C), w_qkv, w_qkv.T, w_proj)

    back = branch.reshape(TYPES, WW, WZ, WH, C).transpose(0, 2, 3, 1, 4).reshape(Z, WH, WW, C)
    back = jnp.roll(back, WZ // 2, axis=0)
    west = shifted(back[:, :half_r, half_c:], 1, 0)
    north = shifted(back[:, half_r:, :half_c], 0, 1)
    far = shifted(back[:, half_r:, half_c:], 1, 1)
    upper = jnp.concatenate([far, north], axis=2)
    lower = jnp.concatenate([west, back[:, :half_r, :half_c]], axis=2)
    back = jnp.concatenate([upper, lower], axis=1)
    d_field = (cotangent.astype(F32) + back.astype(F32)).astype(BF16)

    codes = codes.reshape(GROUPS * 24, 3, 128).transpose(1, 0, 2)
    packed = pl.pallas_call(
        table_kernel,
        out_shape=jax.ShapeDtypeStruct((TROWS, 128), BF16),
        scratch_shapes=[pltpu.VMEM((3 * PAIRS, GROUPS, 128), F32)],
        compiler_params=pltpu.CompilerParams(vmem_limit_bytes=40 * 2**20),
        name="table_grads",
    )(codes, inverse)

    lats, lons = lax.axis_size("lat"), lax.axis_size("lon")
    w_rows, t_rows = WROWS // lats, TROWS // lons
    piece = added(exchange(weights.reshape(lats, w_rows, 128), "lat"))
    piece = jnp.pad(piece, ((0, 80 - w_rows), (0, 0)))
    small = 80 // lons
    sent = jnp.concatenate(
        [packed.reshape(lons, t_rows, 128), piece.reshape(lons, small, 128)], axis=1
    )
    mine = added(exchange(sent, "lon"))
    got = spread(mine, "lon")
    packed = got[:, :t_rows].reshape(TROWS, 128)
    piece = got[:, t_rows:].reshape(80, 128)[:w_rows]
    weights = spread(piece, "lat").reshape(WROWS, 128)

    tokens_total = Z * valid_rows.shape[0] * lons * WW
    d_gain, d_wqkv, d_wproj, d_table = pl.pallas_call(
        functools.partial(finish_kernel, tokens_total**-0.5, (lons * WW) ** -0.5),
        out_shape=(
            jax.ShapeDtypeStruct((1, C), F32),
            jax.ShapeDtypeStruct((C, 3 * C), F32),
            jax.ShapeDtypeStruct((C, C), F32),
            jax.ShapeDtypeStruct((TYPES, HEADS, POS), F32),
        ),
        compiler_params=pltpu.CompilerParams(vmem_limit_bytes=40 * 2**20),
        name="unpack",
    )(weights, packed)
    return d_field, d_gain.reshape(C), d_wqkv, d_wproj, d_table


def solution(mesh):
    field = P(None, "lat", "lon", None)
    table = P("lat", None, None)
    return jax.shard_map(
        per_device,
        mesh=mesh,
        in_specs=(field, field, P(), P(), P(), table, P(), P()),
        out_specs=(field, P(), P(), P(), table),
        check_vma=False,
    )
```

```python
import functools

import jax
import jax.numpy as jnp
from jax import lax
from jax.experimental import pallas as pl
from jax.experimental.pallas import tpu as pltpu
from jax.sharding import PartitionSpec as P

HEADS = 6
Z = 8
WZ = 2
WH = 6
WW = 12
WIN = 144
POS = 3312
C = 192
HD = 32
TYPES = 4
GROUPS = TYPES * HEADS
PAIRS = 12
SPAN = 2 * WW - 1
LANES = 384
CHUNKS = 26
TAIL = SPAN * PAIRS - 256
SCALE = HD**-0.5
NEG = -1e30
WROWS = 1280
TROWS = 640
AHEAD, BEHIND = 2, 1
F32 = jnp.float32
BF16 = jnp.bfloat16


def nn(left, right):
    return lax.dot_general(left, right, (((1,), (0,)), ((), ())), preferred_element_type=F32)


def nt(left, right):
    return lax.dot_general(left, right, (((1,), (1,)), ((), ())), preferred_element_type=F32)


def bias_kernel(base, position, table, bias, inverse, sheet, codes):
    for head in range(HEADS):
        sheet[head * TYPES : (head + 1) * TYPES, :POS] = table[head]
    sheet[:, POS:] = jnp.zeros((GROUPS, CHUNKS * 128 - POS), F32)
    token = lax.broadcasted_iota(jnp.int32, (WIN, WIN), 0)
    col = lax.div(token, PAIRS)
    place = token - col * PAIRS
    row, level = lax.shift_right_logical(place, 1), lax.bitwise_and(place, 1)
    natural = level * (WH * WW) + row * WW + col
    order = jnp.where(lax.broadcasted_iota(jnp.int32, (WIN, WIN), 1) == natural, 1.0, 0.0)
    order = order.astype(BF16)
    entries = position[...]
    digits = []
    for digit in (lax.shift_right_arithmetic(entries, 7), lax.bitwise_and(entries, 127)):
        turned = nt(order, digit.astype(F32).astype(BF16)).astype(BF16)
        digits.append(nt(turned, order))
    whole_index = digits[0] * 128.0 + digits[1]
    pieces = [
        whole_index[(WW - 1 - gap) * PAIRS : (WW - gap) * PAIRS, :PAIRS] for gap in range(WW - 1)
    ]
    pieces.append(whole_index[:PAIRS, :])
    pieces.append(jnp.full((PAIRS, LANES - SPAN * PAIRS), -1.0, F32))
    index = jnp.concatenate(pieces, axis=1).astype(jnp.int32)

    tails = [
        jnp.concatenate(
            [index[place : place + 1, 256 : 256 + TAIL] for place in range(6 * half, 6 * half + 6)]
            + [jnp.full((1, 128 - 6 * TAIL), -1, jnp.int32)],
            axis=1,
        )
        for half in range(2)
    ]

    def lookup(entry):
        entry = jnp.broadcast_to(entry, (GROUPS, 128))
        high = lax.shift_right_arithmetic(entry, 7)
        low = lax.bitwise_and(entry, 127)
        found = jnp.zeros((GROUPS, 128), F32)
        for chunk in range(CHUNKS):
            source = sheet[:, chunk * 128 : (chunk + 1) * 128]
            found = jnp.where(high == chunk, jnp.take_along_axis(source, low, axis=1), found)
        return found

    last = [lookup(tail) for tail in tails]
    for place in range(PAIRS):
        parts = [lookup(index[place : place + 1, col * 128 : (col + 1) * 128]) for col in range(2)]
        turn = place % 6 * TAIL
        tail = last[place // 6]
        parts.append(tail if turn == 0 else pltpu.roll(tail, 128 - turn, 1))
        row = jnp.concatenate(parts, axis=1)
        moved = pltpu.roll(row, PAIRS, 1)
        for col in range(3):
            at = slice(col * 128, (col + 1) * 128)
            codes[col, pl.ds(place, GROUPS, stride=24), :] = row[:, at]
            codes[col, pl.ds(PAIRS + place, GROUPS, stride=24), :] = moved[:, at]

    first = base[0]
    lat_total = base.shape[0] - 2

    def places(shape, axis):
        token = lax.broadcasted_iota(jnp.int32, shape, axis)
        place = lax.rem(token, PAIRS)
        row, level = lax.shift_right_logical(place, 1), lax.bitwise_and(place, 1)
        return row, level, (first + row >= lat_total - WH // 2).astype(jnp.int32)

    key_row, key_level, key_late = places((WIN, 1), 0)
    _, query_level, query_late = places((1, WIN), 1)
    good = jnp.zeros((WIN, 1), jnp.int32)
    for row in range(WH):
        valid = base[2 + lax.rem(first + row + WH // 2, lat_total)]
        good = jnp.where(key_row == row, valid, good)
    rows_allowed = (key_late == query_late) & (good > 0)
    top_allowed = rows_allowed & (key_level == query_level)
    for window in range(TYPES):
        allowed = top_allowed if window == TYPES - 1 else rows_allowed
        for head in range(HEADS):
            group = head * TYPES + window
            block = jnp.concatenate(
                [codes[col, group * 24 : (group + 1) * 24, :] for col in range(3)], axis=1
            )
            pieces = []
            for step in range(WW // 2):
                turned = pltpu.roll(block, LANES - (132 - 24 * step), 1)
                pieces.append(turned[:, :WIN])
            full = jnp.concatenate(pieces, axis=0)
            bias[group] = jnp.where(allowed, full, NEG)
    total = jnp.zeros((64, 128), F32)
    lane = lax.broadcasted_iota(jnp.int32, (32, 128), 1).astype(F32)
    tall = lax.broadcasted_iota(jnp.int32, (32, 128), 0)
    deep = lax.broadcasted_iota(jnp.int32, (128, 128), 0)
    rows = [index[place : place + 1, at : at + 128] for place in range(PAIRS) for at in (0, 128)]
    for chunk, entry in enumerate(rows + tails):
        high = lax.shift_right_arithmetic(entry, 7)
        low = lax.bitwise_and(entry, 127)
        hit = high == tall
        left = jnp.concatenate([jnp.where(hit, float(chunk), 0.0), jnp.where(hit, lane, 0.0)], axis=0)
        right = jnp.where(deep == low, 1.0, 0.0).astype(BF16)
        total = total + nt(left.astype(BF16), right)
    inverse[...] = total.astype(jnp.int32)


def window_kernel(
    base,
    x_own,
    dy_own,
    east,
    south,
    corner,
    bias,
    gain,
    wq,
    wp,
    back_own,
    back_east,
    back_south,
    back_corner,
    codes,
    kept,
    given,
    natural,
    windows,
    weights,
):
    half_r, half_c = WH // 2, WW // 2
    for array, own in enumerate((x_own, dy_own)):
        for col in range(WW):
            for row in range(WH):
                if col < half_c:
                    if row < half_r:
                        tile = own[row, col]
                    else:
                        tile = south[array, row - half_r, col]
                elif row < half_r:
                    tile = east[array, row, col - half_c]
                else:
                    tile = corner[array, row - half_r, col - half_c]
                tile = tile.astype(F32)
                at = (col * WH + row) * Z
                natural[2 * array, at : at + Z, :] = tile[:, :128]
                natural[2 * array + 1, at : at + Z, :64] = tile[:, 128:]
    for part in range(4):
        for window in range(TYPES):
            for level in range(WZ):
                source = natural[part, pl.ds((WZ * window + level + 1) % Z, 72, stride=Z), :]
                windows[part, pl.ds(window * WIN + level, 72, stride=WZ), :] = source

    tokens = jnp.concatenate([windows[0], windows[1][:, :64]], axis=1)
    grads_all = jnp.concatenate([windows[2], windows[3][:, :64]], axis=1).astype(BF16)
    average = jnp.mean(tokens, axis=1, keepdims=True)
    centred = tokens - average
    inv_std_all = lax.rsqrt(jnp.mean(centred * centred, axis=1, keepdims=True) + 1e-5)
    normed_all = centred * inv_std_all
    gains = gain[...]
    hidden_all = (normed_all * gains).astype(BF16)
    wq_t = wq[...].astype(F32).T.astype(BF16)
    key_value = nn(hidden_all, wq[:, C:]).astype(BF16)

    totals = [None, None, None]

    def prepare(window):
        span = slice(window * WIN, (window + 1) * WIN)
        state = {"span": span, "hidden": hidden_all[span], "grads": grads_all[span]}
        state["keys"], state["values"] = key_value[span, :C], key_value[span, C:]
        state["qkv_t"] = nt(wq_t, state["hidden"]).astype(BF16)
        state["datt_t"] = nt(wp[...], state["grads"]).astype(BF16)
        for name in ("att", "dq", "dk", "dv"):
            state[name] = []
        return state

    def features(state, head):
        part = [state["qkv_t"][at + head * HD : at + (head + 1) * HD] for at in (0, C, 2 * C)]
        return part + [state["datt_t"][head * HD : (head + 1) * HD]]

    def products(state, head):
        q_t, _, _, a_t = features(state, head)
        scores = nn(state["keys"][:, head * HD : (head + 1) * HD], q_t)
        d_probs = nn(state["values"][:, head * HD : (head + 1) * HD], a_t)
        return scores, d_probs

    def softmax(window, head, scores, d_probs):
        scores = scores * SCALE + bias[head * TYPES + window]
        raised = jnp.exp(scores - jnp.max(scores, axis=0, keepdims=True))
        probs = raised * (1.0 / jnp.sum(raised, axis=0, keepdims=True))
        d_scores = probs * (d_probs - jnp.sum(d_probs * probs, axis=0, keepdims=True))
        return probs.astype(BF16), d_scores

    def gradients(state, window, head, probs_b, d_scores):
        q_t, k_t, v_t, a_t = features(state, head)
        group = head * TYPES + window
        d_scores_b = (d_scores * SCALE).astype(BF16)
        state["att"].append(nn(v_t, probs_b).astype(BF16))
        state["dq"].append(nn(k_t, d_scores_b).astype(BF16))
        state["dk"].append(nt(q_t, d_scores_b).astype(BF16))
        state["dv"].append(nt(a_t, probs_b).astype(BF16))
        folded = None
        for part in range(WW // 2):
            rows = d_scores[part * 24 : (part + 1) * 24]
            rows = jnp.concatenate([rows, jnp.zeros((24, LANES - WIN), F32)], axis=1)
            folded = rows if part == 0 else pltpu.roll(folded, 24, 1) + rows
        folded = pltpu.roll(folded, PAIRS, 1)
        for col in range(3):
            codes[col, group * 24 : (group + 1) * 24, :] = folded[:, col * 128 : (col + 1) * 128]

    def close(state):
        span, hidden, grads = state["span"], state["hidden"], state["grads"]
        normed, inv_std = normed_all[span], inv_std_all[span]
        att_t = jnp.concatenate(state["att"], axis=0)
        dqkv_t = jnp.concatenate(state["dq"] + state["dk"] + state["dv"], axis=0)
        d_hidden = nn(wq[...], dqkv_t).T
        parts = (
            nn(dqkv_t, hidden),
            nn(att_t, grads),
            jnp.sum(d_hidden * normed, axis=0, keepdims=True),
        )
        for at, part in enumerate(parts):
            totals[at] = part if totals[at] is None else totals[at] + part
        d_norm = d_hidden * gains
        branch = inv_std * (
            d_norm
            - jnp.mean(d_norm, axis=1, keepdims=True)
            - normed * jnp.mean(d_norm * normed, axis=1, keepdims=True)
        )
        windows[0, span, :] = branch[:, :128]
        windows[1, span, :64] = branch[:, 128:]

    states, first, second = {}, {}, {}
    for step in range(GROUPS + AHEAD + BEHIND):
        if step < GROUPS:
            window, head = divmod(step, HEADS)
            if head == 0:
                states[window] = prepare(window)
            first[step] = products(states[window], head)
        at = step - AHEAD
        if 0 <= at < GROUPS:
            window, head = divmod(at, HEADS)
            second[at] = softmax(window, head, *first.pop(at))
        at = step - AHEAD - BEHIND
        if at >= 0:
            window, head = divmod(at, HEADS)
            gradients(states[window], window, head, *second.pop(at))
            if head == HEADS - 1:
                close(states.pop(window))
    dw, dp, dg = totals

    for part in range(2):
        for window in range(TYPES):
            for level in range(WZ):
                source = windows[part, pl.ds(window * WIN + level, 72, stride=WZ), :]
                natural[part, pl.ds((WZ * window + level + 1) % Z, 72, stride=Z), :] = source
    for col in range(WW):
        for row in range(WH):
            at = (col * WH + row) * Z
            tile = jnp.concatenate(
                [natural[0, at : at + Z, :], natural[1, at : at + Z, :64]], axis=1
            )
            if row < half_r:
                target = back_own if col < half_c else back_east
            else:
                target = back_south if col < half_c else back_corner
            target[row % half_r, col % half_c] = tile.astype(BF16)

    weights[0:576, :] = dw[:, :128].astype(BF16)
    weights[576:864, :] = jnp.concatenate([dw[:288, 128:], dw[288:, 128:]], axis=1).astype(BF16)
    weights[864:1056, :] = dp[:, :128].astype(BF16)
    weights[1056:1152, :] = jnp.concatenate([dp[:96, 128:], dp[96:, 128:]], axis=1).astype(BF16)
    wide = jnp.concatenate([dg, jnp.zeros((1, 64), F32)], axis=1)
    last = jnp.concatenate([wide[:, :128], wide[:, 128:], jnp.zeros((126, 128), F32)], axis=0)
    weights[1152:1280, :] = last.astype(BF16)
    core = base[1]
    half = WROWS // 2
    kept[...] = weights[pl.ds(pl.multiple_of(core * half, half), half), :]
    given[...] = weights[pl.ds(pl.multiple_of((1 - core) * half, half), half), :]


def table_kernel(codes, inverse, packed, rows):
    lane = lax.broadcasted_iota(jnp.int32, (GROUPS, 128), 1)
    tails = [jnp.zeros((GROUPS, 128), F32), jnp.zeros((GROUPS, 128), F32)]
    for place in range(PAIRS):
        above = jnp.concatenate(
            [codes[col, pl.ds(place, GROUPS, stride=24), :] for col in range(3)], axis=1
        )
        below = jnp.concatenate(
            [codes[col, pl.ds(PAIRS + place, GROUPS, stride=24), :] for col in range(3)], axis=1
        )
        both = above + pltpu.roll(below, LANES - PAIRS, 1)
        rows[2 * place] = both[:, :128]
        rows[2 * place + 1] = both[:, 128:256]
        turn = place % 6 * TAIL
        tail = both[:, 256:]
        tail = tail if turn == 0 else pltpu.roll(tail, turn, 1)
        inside = (lane >= turn) & (lane < turn + TAIL)
        tails[place // 6] = jnp.where(inside, tail, tails[place // 6])
    rows[2 * PAIRS] = tails[0]
    rows[2 * PAIRS + 1] = tails[1]
    for chunk in range(CHUNKS):
        source = jnp.broadcast_to(inverse[chunk : chunk + 1, :], (GROUPS, 128))
        low = jnp.broadcast_to(inverse[32 + chunk : 33 + chunk, :], (GROUPS, 128))
        found = jnp.zeros((GROUPS, 128), F32)
        for at in range(CHUNKS):
            found = jnp.where(source == at, jnp.take_along_axis(rows[at], low, axis=1), found)
        packed[chunk * GROUPS : (chunk + 1) * GROUPS, :] = found.astype(BF16)
    packed[CHUNKS * GROUPS :, :] = jnp.zeros((TROWS - CHUNKS * GROUPS, 128), BF16)


def finish_kernel(
    grad_scale, table_scale, base, kept, taken, packed_t, d_gain, d_wqkv, d_wproj, d_table, weights
):
    core = base[1]
    half = WROWS // 2
    weights[pl.ds(pl.multiple_of(core * half, half), half), :] = kept[...]
    weights[pl.ds(pl.multiple_of((1 - core) * half, half), half), :] = taken[...]
    scaled = weights[...].astype(F32) * grad_scale
    side = scaled[576:864]
    right = jnp.concatenate([side[:, :64], side[:, 64:]], axis=0)
    d_wqkv[...] = jnp.concatenate([scaled[:576], right], axis=1).T
    side = scaled[1056:1152]
    right = jnp.concatenate([side[:, :64], side[:, 64:]], axis=0)
    d_wproj[...] = jnp.concatenate([scaled[864:1056], right], axis=1)
    d_gain[...] = jnp.concatenate([scaled[1152:1153], scaled[1153:1154, :64]], axis=1)
    for chunk in range(CHUNKS):
        part = packed_t[chunk * 24 : (chunk + 1) * 24, :].astype(F32) * table_scale
        width = min(128, POS - chunk * 128)
        for head in range(HEADS):
            d_table[head, :, chunk * 128 : chunk * 128 + width] = part[
                head * TYPES : (head + 1) * TYPES, :width
            ]


def shifted(value, steps_lon, steps_lat):
    lons, lats = lax.axis_size("lon"), lax.axis_size("lat")
    pairs = [
        (i * lats + j, (i + steps_lon) % lons * lats + (j + steps_lat) % lats)
        for i in range(lons)
        for j in range(lats)
    ]
    return lax.ppermute(value, ("lon", "lat"), pairs)


def other_core(value):
    count = lax.axis_size("lat")
    return lax.ppermute(value, "lat", [(i, i ^ 1) for i in range(count)])


def exchange(value, axis, groups=None):
    return lax.all_to_all(value, axis, 0, 0, axis_index_groups=groups)


def added(pieces):
    return jnp.sum(pieces.astype(F32), axis=0).astype(BF16)


def spread(piece, axis, groups=None):
    count = lax.axis_size(axis) if groups is None else len(groups[0])
    return exchange(jnp.broadcast_to(piece[None], (count,) + piece.shape), axis, groups)


def call(kernel, name, out_shape, scratch=(), in_specs=None, limit=16, micros=2):
    extra = {} if in_specs is None else {"in_specs": in_specs}
    return pl.pallas_call(
        kernel,
        out_shape=out_shape,
        scratch_shapes=list(scratch),
        compiler_params=pltpu.CompilerParams(vmem_limit_bytes=limit * 2**20),
        name=name,
        cost_estimate=pl.CostEstimate(
            flops=micros * 10**9, bytes_accessed=micros * 3 * 10**6, transcendentals=0
        ),
        **extra,
    )


def per_device(x_field, cotangent, gain, w_qkv, w_proj, bias_table, position_index, valid_rows):
    half_r, half_c = WH // 2, WW // 2
    x_own = x_field.transpose(1, 2, 0, 3)
    dy_own = cotangent.transpose(1, 2, 0, 3)

    def both(rows, cols):
        return jnp.stack([x_own[rows, cols], dy_own[rows, cols]])

    top, bottom = slice(0, half_r), slice(half_r, WH)
    left, right = slice(0, half_c), slice(half_c, WW)
    east = shifted(both(bottom, left), -1, 0)
    corner = shifted(both(top, left), -1, -1)
    south = shifted(both(top, right), 0, -1)

    lat = lax.axis_index("lat").astype(jnp.int32)
    base = jnp.concatenate([jnp.stack([lat * WH, lat % 2]), valid_rows])
    vmem, smem = pl.BlockSpec(memory_space=pltpu.VMEM), pl.BlockSpec(memory_space=pltpu.SMEM)
    quarter = jax.ShapeDtypeStruct((half_r, half_c, Z, C), BF16)
    bias, inverse = call(
        bias_kernel,
        "bias_lookup",
        (
            jax.ShapeDtypeStruct((GROUPS, WIN, WIN), F32),
            jax.ShapeDtypeStruct((64, 128), jnp.int32),
        ),
        [
            pltpu.VMEM((GROUPS, CHUNKS * 128), F32),
            pltpu.VMEM((3, GROUPS * 24, 128), F32),
        ],
        [smem, vmem, vmem],
        micros=6,
    )(base, position_index, bias_table.transpose(1, 0, 2))

    half_w = jax.ShapeDtypeStruct((WROWS // 2, 128), BF16)
    back_own, back_east, back_south, back_corner, codes, kept, given = call(
        window_kernel,
        "window_grads",
        (
            quarter,
            quarter,
            quarter,
            quarter,
            jax.ShapeDtypeStruct((3, GROUPS * 24, 128), F32),
            half_w,
            half_w,
        ),
        [
            pltpu.VMEM((4, 576, 128), F32),
            pltpu.VMEM((4, 576, 128), F32),
            pltpu.VMEM((WROWS, 128), BF16),
        ],
        [smem] + [vmem] * 9,
        limit=24,
        micros=7,
    )(
        base,
        x_own[bottom, right],
        dy_own[bottom, right],
        east,
        south,
        corner,
        bias,
        gain.reshape(1, C),
        w_qkv,
        w_proj,
    )

    taken = other_core(given)
    west = shifted(back_east, 1, 0)
    far = shifted(back_corner, 1, 1)
    north = shifted(back_south, 0, 1)
    packed = call(
        table_kernel,
        "table_grads",
        jax.ShapeDtypeStruct((TROWS, 128), BF16),
        [pltpu.VMEM((CHUNKS, GROUPS, 128), F32)],
    )(codes, inverse)

    lats, lons = lax.axis_size("lat"), lax.axis_size("lon")
    w_rows, t_rows = WROWS // 2 // lons, TROWS // lons
    mine = (kept.astype(F32) + taken.astype(F32)).astype(BF16).reshape(lons, w_rows, 128)
    sent = jnp.concatenate([mine, packed.reshape(lons, t_rows, 128)], axis=1)
    summed = added(exchange(sent, "lon"))
    summed, west, far, north = lax.optimization_barrier((summed, west, far, north))
    same_core = [list(range(start, lats, 2)) for start in range(2)]
    piece = added(spread(summed[:w_rows], "lat", same_core))
    got = spread(jnp.concatenate([piece, summed[w_rows:]], axis=0), "lon")
    packed = got[:, w_rows:].reshape(TROWS, 128)
    kept = got[:, :w_rows].reshape(WROWS // 2, 128)
    taken = other_core(kept)

    upper = jnp.concatenate([far, north], axis=1)
    lower = jnp.concatenate([west, back_own], axis=1)
    back = jnp.concatenate([upper, lower], axis=0)
    d_field = (dy_own.astype(F32) + back.astype(F32)).astype(BF16).transpose(2, 0, 1, 3)

    tokens_total = Z * valid_rows.shape[0] * lons * WW
    d_gain, d_wqkv, d_wproj, d_table = call(
        functools.partial(finish_kernel, tokens_total**-0.5, (lons * WW) ** -0.5),
        "unpack",
        (
            jax.ShapeDtypeStruct((1, C), F32),
            jax.ShapeDtypeStruct((C, 3 * C), F32),
            jax.ShapeDtypeStruct((C, C), F32),
            jax.ShapeDtypeStruct((HEADS, TYPES, POS), F32),
        ),
        [pltpu.VMEM((WROWS, 128), BF16)],
        [smem] + [vmem] * 3,
    )(base, kept, taken, packed)
    return d_field, d_gain.reshape(C), d_wqkv, d_wproj, d_table.transpose(1, 0, 2)


def solution(mesh):
    field = P(None, "lat", "lon", None)
    table = P("lat", None, None)
    return jax.shard_map(
        per_device,
        mesh=mesh,
        in_specs=(field, field, P(), P(), P(), table, P(), P()),
        out_specs=(field, P(), P(), P(), table),
        check_vma=False,
    )
```

```python
import functools
import itertools

import jax
import jax.numpy as jnp
from jax import lax
from jax.experimental import pallas as pl
from jax.experimental.pallas import tpu as pltpu
from jax.sharding import PartitionSpec as P

HEADS = 6
Z = 8
WZ = 2
WH = 6
WW = 12
WIN = 144
POS = 3312
C = 192
HD = 32
TYPES = 4
GROUPS = TYPES * HEADS
PAIRS = 12
SPAN = 2 * WW - 1
LANES = 384
CHUNKS = 26
TAIL = SPAN * PAIRS - 256
SCALE = HD**-0.5
NEG = -1e30
WROWS = 1280
TROWS = 640
AHEAD, BEHIND = 2, 1
F32 = jnp.float32
BF16 = jnp.bfloat16


def nn(left, right):
    return lax.dot_general(left, right, (((1,), (0,)), ((), ())), preferred_element_type=F32)


def nt(left, right):
    return lax.dot_general(left, right, (((1,), (1,)), ((), ())), preferred_element_type=F32)


def bias_kernel(base, position, table, bias, inverse, sheet, codes):
    for head in range(HEADS):
        sheet[head * TYPES : (head + 1) * TYPES, :POS] = table[head]
    sheet[:, POS:] = jnp.zeros((GROUPS, CHUNKS * 128 - POS), F32)
    token = lax.broadcasted_iota(jnp.int32, (WIN, WIN), 0)
    col = lax.div(token, PAIRS)
    place = token - col * PAIRS
    row, level = lax.shift_right_logical(place, 1), lax.bitwise_and(place, 1)
    natural = level * (WH * WW) + row * WW + col
    order = jnp.where(lax.broadcasted_iota(jnp.int32, (WIN, WIN), 1) == natural, 1.0, 0.0)
    order = order.astype(BF16)
    entries = position[...]
    digits = []
    for digit in (lax.shift_right_arithmetic(entries, 7), lax.bitwise_and(entries, 127)):
        turned = nt(order, digit.astype(F32).astype(BF16)).astype(BF16)
        digits.append(nt(turned, order))
    whole_index = digits[0] * 128.0 + digits[1]
    pieces = [
        whole_index[(WW - 1 - gap) * PAIRS : (WW - gap) * PAIRS, :PAIRS] for gap in range(WW - 1)
    ]
    pieces.append(whole_index[:PAIRS, :])
    pieces.append(jnp.full((PAIRS, LANES - SPAN * PAIRS), -1.0, F32))
    index = jnp.concatenate(pieces, axis=1).astype(jnp.int32)

    tails = [
        jnp.concatenate(
            [index[place : place + 1, 256 : 256 + TAIL] for place in range(6 * half, 6 * half + 6)]
            + [jnp.full((1, 128 - 6 * TAIL), -1, jnp.int32)],
            axis=1,
        )
        for half in range(2)
    ]

    def lookup(entry):
        entry = jnp.broadcast_to(entry, (GROUPS, 128))
        high = lax.shift_right_arithmetic(entry, 7)
        low = lax.bitwise_and(entry, 127)
        found = jnp.zeros((GROUPS, 128), F32)
        for chunk in range(CHUNKS):
            source = sheet[:, chunk * 128 : (chunk + 1) * 128]
            found = jnp.where(high == chunk, jnp.take_along_axis(source, low, axis=1), found)
        return found

    last = [lookup(tail) for tail in tails]
    for place in range(PAIRS):
        parts = [lookup(index[place : place + 1, col * 128 : (col + 1) * 128]) for col in range(2)]
        turn = place % 6 * TAIL
        tail = last[place // 6]
        parts.append(tail if turn == 0 else pltpu.roll(tail, 128 - turn, 1))
        row = jnp.concatenate(parts, axis=1)
        moved = pltpu.roll(row, PAIRS, 1)
        for col in range(3):
            at = slice(col * 128, (col + 1) * 128)
            codes[col, pl.ds(place, GROUPS, stride=24), :] = row[:, at]
            codes[col, pl.ds(PAIRS + place, GROUPS, stride=24), :] = moved[:, at]

    first = base[0]
    lat_total = base.shape[0] - 2

    def places(shape, axis):
        token = lax.broadcasted_iota(jnp.int32, shape, axis)
        place = lax.rem(token, PAIRS)
        row, level = lax.shift_right_logical(place, 1), lax.bitwise_and(place, 1)
        return row, level, (first + row >= lat_total - WH // 2).astype(jnp.int32)

    key_row, key_level, key_late = places((WIN, 1), 0)
    _, query_level, query_late = places((1, WIN), 1)
    good = jnp.zeros((WIN, 1), jnp.int32)
    for row in range(WH):
        valid = base[2 + lax.rem(first + row + WH // 2, lat_total)]
        good = jnp.where(key_row == row, valid, good)
    rows_allowed = (key_late == query_late) & (good > 0)
    top_allowed = rows_allowed & (key_level == query_level)
    for window in range(TYPES):
        allowed = top_allowed if window == TYPES - 1 else rows_allowed
        for head in range(HEADS):
            group = head * TYPES + window
            block = jnp.concatenate(
                [codes[col, group * 24 : (group + 1) * 24, :] for col in range(3)], axis=1
            )
            pieces = []
            for step in range(WW // 2):
                turned = pltpu.roll(block, LANES - (132 - 24 * step), 1)
                pieces.append(turned[:, :WIN])
            full = jnp.concatenate(pieces, axis=0)
            bias[group] = jnp.where(allowed, full, NEG)
    total = jnp.zeros((64, 128), F32)
    lane = lax.broadcasted_iota(jnp.int32, (32, 128), 1).astype(F32)
    tall = lax.broadcasted_iota(jnp.int32, (32, 128), 0)
    deep = lax.broadcasted_iota(jnp.int32, (128, 128), 0)
    rows = [index[place : place + 1, at : at + 128] for place in range(PAIRS) for at in (0, 128)]
    for chunk, entry in enumerate(rows + tails):
        high = lax.shift_right_arithmetic(entry, 7)
        low = lax.bitwise_and(entry, 127)
        hit = high == tall
        left = jnp.concatenate([jnp.where(hit, float(chunk), 0.0), jnp.where(hit, lane, 0.0)], axis=0)
        right = jnp.where(deep == low, 1.0, 0.0).astype(BF16)
        total = total + nt(left.astype(BF16), right)
    inverse[...] = total.astype(jnp.int32)


def window_kernel(
    base,
    own,
    east,
    south,
    corner,
    bias,
    gain,
    wq,
    wp,
    back_own,
    back_east,
    back_south,
    back_corner,
    codes,
    kept,
    given,
    natural,
    windows,
    weights,
):
    half_r, half_c = WH // 2, WW // 2
    for col in range(WW):
        for row in range(WH):
            if row < half_r:
                source = own if col < half_c else east
            else:
                source = south if col < half_c else corner
            tile = source[row % half_r, col % half_c].astype(F32)
            at = (col * WH + row) * Z
            for part in range(3):
                natural[part, at : at + Z, :] = tile[:, part * 128 : (part + 1) * 128]
    for part in range(3):
        for window in range(TYPES):
            for level in range(WZ):
                source = natural[part, pl.ds((WZ * window + level + 1) % Z, 72, stride=Z), :]
                windows[part, pl.ds(window * WIN + level, 72, stride=WZ), :] = source

    tokens = jnp.concatenate([windows[0], windows[1][:, :64]], axis=1)
    grads_all = jnp.concatenate([windows[1][:, 64:], windows[2]], axis=1).astype(BF16)
    average = jnp.mean(tokens, axis=1, keepdims=True)
    centred = tokens - average
    inv_std_all = lax.rsqrt(jnp.mean(centred * centred, axis=1, keepdims=True) + 1e-5)
    normed_all = centred * inv_std_all
    gains = gain[...]
    hidden_all = (normed_all * gains).astype(BF16)
    wq_t = wq[...].astype(F32).T.astype(BF16)
    key_value = nn(hidden_all, wq[:, C:]).astype(BF16)

    totals = [None, None, None]

    def prepare(window):
        span = slice(window * WIN, (window + 1) * WIN)
        state = {"span": span, "hidden": hidden_all[span], "grads": grads_all[span]}
        state["keys"], state["values"] = key_value[span, :C], key_value[span, C:]
        state["qkv_t"] = nt(wq_t, state["hidden"]).astype(BF16)
        state["datt_t"] = nt(wp[...], state["grads"]).astype(BF16)
        for name in ("att", "dq", "dk", "dv"):
            state[name] = []
        return state

    def features(state, head):
        part = [state["qkv_t"][at + head * HD : at + (head + 1) * HD] for at in (0, C, 2 * C)]
        return part + [state["datt_t"][head * HD : (head + 1) * HD]]

    def products(state, head):
        q_t, _, _, a_t = features(state, head)
        scores = nn(state["keys"][:, head * HD : (head + 1) * HD], q_t)
        d_probs = nn(state["values"][:, head * HD : (head + 1) * HD], a_t)
        return scores, d_probs

    def softmax(window, head, scores, d_probs):
        scores = scores * SCALE + bias[head * TYPES + window]
        raised = jnp.exp(scores - jnp.max(scores, axis=0, keepdims=True))
        probs = raised * (1.0 / jnp.sum(raised, axis=0, keepdims=True))
        d_scores = probs * (d_probs - jnp.sum(d_probs * probs, axis=0, keepdims=True))
        return probs.astype(BF16), d_scores

    def gradients(state, window, head, probs_b, d_scores):
        q_t, k_t, v_t, a_t = features(state, head)
        group = head * TYPES + window
        d_scores_b = (d_scores * SCALE).astype(BF16)
        state["att"].append(nn(v_t, probs_b).astype(BF16))
        state["dq"].append(nn(k_t, d_scores_b).astype(BF16))
        state["dk"].append(nt(q_t, d_scores_b).astype(BF16))
        state["dv"].append(nt(a_t, probs_b).astype(BF16))
        folded = None
        for part in range(WW // 2):
            rows = d_scores[part * 24 : (part + 1) * 24]
            rows = jnp.concatenate([rows, jnp.zeros((24, LANES - WIN), F32)], axis=1)
            folded = rows if part == 0 else pltpu.roll(folded, 24, 1) + rows
        folded = pltpu.roll(folded, PAIRS, 1)
        for col in range(3):
            codes[col, group * 24 : (group + 1) * 24, :] = folded[:, col * 128 : (col + 1) * 128]

    def close(state):
        span, hidden, grads = state["span"], state["hidden"], state["grads"]
        normed, inv_std = normed_all[span], inv_std_all[span]
        att_t = jnp.concatenate(state["att"], axis=0)
        dqkv_t = jnp.concatenate(state["dq"] + state["dk"] + state["dv"], axis=0)
        d_hidden = nn(wq[...], dqkv_t).T
        parts = (
            nn(dqkv_t, hidden),
            nn(att_t, grads),
            jnp.sum(d_hidden * normed, axis=0, keepdims=True),
        )
        for at, part in enumerate(parts):
            totals[at] = part if totals[at] is None else totals[at] + part
        d_norm = d_hidden * gains
        branch = inv_std * (
            d_norm
            - jnp.mean(d_norm, axis=1, keepdims=True)
            - normed * jnp.mean(d_norm * normed, axis=1, keepdims=True)
        )
        windows[0, span, :] = branch[:, :128]
        windows[1, span, :64] = branch[:, 128:]

    states, first, second = {}, {}, {}
    for step in range(GROUPS + AHEAD + BEHIND):
        if step < GROUPS:
            window, head = divmod(step, HEADS)
            if head == 0:
                states[window] = prepare(window)
            first[step] = products(states[window], head)
        at = step - AHEAD
        if 0 <= at < GROUPS:
            window, head = divmod(at, HEADS)
            second[at] = softmax(window, head, *first.pop(at))
        at = step - AHEAD - BEHIND
        if at >= 0:
            window, head = divmod(at, HEADS)
            gradients(states[window], window, head, *second.pop(at))
            if head == HEADS - 1:
                close(states.pop(window))
    dw, dp, dg = totals

    for part in range(2):
        for window in range(TYPES):
            for level in range(WZ):
                source = windows[part, pl.ds(window * WIN + level, 72, stride=WZ), :]
                natural[part, pl.ds((WZ * window + level + 1) % Z, 72, stride=Z), :] = source
    for col in range(WW):
        for row in range(WH):
            at = (col * WH + row) * Z
            tile = jnp.concatenate(
                [natural[0, at : at + Z, :], natural[1, at : at + Z, :64]], axis=1
            )
            if row < half_r:
                target = back_own if col < half_c else back_east
            else:
                target = back_south if col < half_c else back_corner
            target[row % half_r, col % half_c] = tile.astype(BF16)

    weights[0:576, :] = dw[:, :128].astype(BF16)
    weights[576:864, :] = jnp.concatenate([dw[:288, 128:], dw[288:, 128:]], axis=1).astype(BF16)
    weights[864:1056, :] = dp[:, :128].astype(BF16)
    weights[1056:1152, :] = jnp.concatenate([dp[:96, 128:], dp[96:, 128:]], axis=1).astype(BF16)
    wide = jnp.concatenate([dg, jnp.zeros((1, 64), F32)], axis=1)
    last = jnp.concatenate([wide[:, :128], wide[:, 128:], jnp.zeros((126, 128), F32)], axis=0)
    weights[1152:1280, :] = last.astype(BF16)
    core = base[1]
    half = WROWS // 2
    kept[...] = weights[pl.ds(pl.multiple_of(core * half, half), half), :]
    given[...] = weights[pl.ds(pl.multiple_of((1 - core) * half, half), half), :]


def table_kernel(codes, inverse, packed, rows):
    lane = lax.broadcasted_iota(jnp.int32, (GROUPS, 128), 1)
    tails = [jnp.zeros((GROUPS, 128), F32), jnp.zeros((GROUPS, 128), F32)]
    for place in range(PAIRS):
        above = jnp.concatenate(
            [codes[col, pl.ds(place, GROUPS, stride=24), :] for col in range(3)], axis=1
        )
        below = jnp.concatenate(
            [codes[col, pl.ds(PAIRS + place, GROUPS, stride=24), :] for col in range(3)], axis=1
        )
        both = above + pltpu.roll(below, LANES - PAIRS, 1)
        rows[2 * place] = both[:, :128]
        rows[2 * place + 1] = both[:, 128:256]
        turn = place % 6 * TAIL
        tail = both[:, 256:]
        tail = tail if turn == 0 else pltpu.roll(tail, turn, 1)
        inside = (lane >= turn) & (lane < turn + TAIL)
        tails[place // 6] = jnp.where(inside, tail, tails[place // 6])
    rows[2 * PAIRS] = tails[0]
    rows[2 * PAIRS + 1] = tails[1]
    for chunk in range(CHUNKS):
        source = jnp.broadcast_to(inverse[chunk : chunk + 1, :], (GROUPS, 128))
        low = jnp.broadcast_to(inverse[32 + chunk : 33 + chunk, :], (GROUPS, 128))
        found = jnp.zeros((GROUPS, 128), F32)
        for at in range(CHUNKS):
            found = jnp.where(source == at, jnp.take_along_axis(rows[at], low, axis=1), found)
        packed[chunk * GROUPS : (chunk + 1) * GROUPS, :] = found.astype(BF16)
    packed[CHUNKS * GROUPS :, :] = jnp.zeros((TROWS - CHUNKS * GROUPS, 128), BF16)


def finish_kernel(
    grad_scale, table_scale, base, kept, taken, packed_t, d_gain, d_wqkv, d_wproj, d_table, weights
):
    core = base[1]
    half = WROWS // 2
    weights[pl.ds(pl.multiple_of(core * half, half), half), :] = kept[...]
    weights[pl.ds(pl.multiple_of((1 - core) * half, half), half), :] = taken[...]
    scaled = weights[...].astype(F32) * grad_scale
    side = scaled[576:864]
    right = jnp.concatenate([side[:, :64], side[:, 64:]], axis=0)
    d_wqkv[...] = jnp.concatenate([scaled[:576], right], axis=1).T
    side = scaled[1056:1152]
    right = jnp.concatenate([side[:, :64], side[:, 64:]], axis=0)
    d_wproj[...] = jnp.concatenate([scaled[864:1056], right], axis=1)
    d_gain[...] = jnp.concatenate([scaled[1152:1153], scaled[1153:1154, :64]], axis=1)
    for chunk in range(CHUNKS):
        part = packed_t[chunk * 24 : (chunk + 1) * 24, :].astype(F32) * table_scale
        width = min(128, POS - chunk * 128)
        for head in range(HEADS):
            d_table[head, :, chunk * 128 : chunk * 128 + width] = part[
                head * TYPES : (head + 1) * TYPES, :width
            ]


def shifted(value, steps_lon, steps_lat):
    lons, lats = lax.axis_size("lon"), lax.axis_size("lat")
    pairs = [
        (i * lats + j, (i + steps_lon) % lons * lats + (j + steps_lat) % lats)
        for i in range(lons)
        for j in range(lats)
    ]
    return lax.ppermute(value, ("lon", "lat"), pairs)


def other_core(value):
    count = lax.axis_size("lat")
    return lax.ppermute(value, "lat", [(i, i ^ 1) for i in range(count)])


def other_half(value):
    count = lax.axis_size("lon")
    return lax.ppermute(value, "lon", [(i, i ^ 1) for i in range(count)])


def peers(names):
    lons, lats = lax.axis_size("lon"), lax.axis_size("lat")
    sizes = {"z": lons // 2, "x_hi": 2, "x_lo": 2, "y": lats // 4, "core": 2}
    others = [name for name in sizes if name not in names]

    def places(wanted):
        return itertools.product(*[range(sizes[name]) for name in wanted])

    def device(at):
        lon = at["z"] * sizes["x_hi"] + at["x_hi"]
        lat = (at["x_lo"] * sizes["y"] + at["y"]) * sizes["core"] + at["core"]
        return lon * lats + lat

    return [
        [device(dict(zip(others, fixed)) | dict(zip(names, place))) for place in places(names)]
        for fixed in places(others)
    ]


def exchange(value, groups):
    return lax.all_to_all(value, ("lon", "lat"), 0, 0, axis_index_groups=groups)


def added(pieces):
    return jnp.sum(pieces.astype(F32), axis=0).astype(BF16)


def spread(piece, groups):
    return exchange(jnp.broadcast_to(piece[None], (len(groups[0]),) + piece.shape), groups)


def call(kernel, name, out_shape, scratch=(), in_specs=None, limit=16, micros=2):
    extra = {} if in_specs is None else {"in_specs": in_specs}
    return pl.pallas_call(
        kernel,
        out_shape=out_shape,
        scratch_shapes=list(scratch),
        compiler_params=pltpu.CompilerParams(vmem_limit_bytes=limit * 2**20),
        name=name,
        cost_estimate=pl.CostEstimate(
            flops=micros * 10**9, bytes_accessed=micros * 3 * 10**6, transcendentals=0
        ),
        **extra,
    )


def per_device(x_field, cotangent, gain, w_qkv, w_proj, bias_table, position_index, valid_rows):
    half_r, half_c = WH // 2, WW // 2
    x_own = x_field.transpose(1, 2, 0, 3)
    dy_own = cotangent.transpose(1, 2, 0, 3)

    def both(rows, cols):
        return jnp.concatenate([x_own[rows, cols], dy_own[rows, cols]], axis=3)

    top, bottom = slice(0, half_r), slice(half_r, WH)
    left, right = slice(0, half_c), slice(half_c, WW)
    east = shifted(both(bottom, left), -1, 0)
    corner = shifted(both(top, left), -1, -1)
    south = shifted(both(top, right), 0, -1)

    lat = lax.axis_index("lat").astype(jnp.int32)
    base = jnp.concatenate([jnp.stack([lat * WH, lat % 2]), valid_rows])
    vmem, smem = pl.BlockSpec(memory_space=pltpu.VMEM), pl.BlockSpec(memory_space=pltpu.SMEM)
    quarter = jax.ShapeDtypeStruct((half_r, half_c, Z, C), BF16)
    bias, inverse = call(
        bias_kernel,
        "bias_lookup",
        (
            jax.ShapeDtypeStruct((GROUPS, WIN, WIN), F32),
            jax.ShapeDtypeStruct((64, 128), jnp.int32),
        ),
        [
            pltpu.VMEM((GROUPS, CHUNKS * 128), F32),
            pltpu.VMEM((3, GROUPS * 24, 128), F32),
        ],
        [smem, vmem, vmem],
        micros=6,
    )(base, position_index, bias_table.transpose(1, 0, 2))

    half_w = jax.ShapeDtypeStruct((WROWS // 2, 128), BF16)
    back_own, back_east, back_south, back_corner, codes, kept, given = call(
        window_kernel,
        "window_grads",
        (
            quarter,
            quarter,
            quarter,
            quarter,
            jax.ShapeDtypeStruct((3, GROUPS * 24, 128), F32),
            half_w,
            half_w,
        ),
        [
            pltpu.VMEM((3, 576, 128), F32),
            pltpu.VMEM((3, 576, 128), F32),
            pltpu.VMEM((WROWS, 128), BF16),
        ],
        [smem] + [vmem] * 8,
        limit=24,
        micros=7,
    )(
        base,
        both(bottom, right),
        east,
        south,
        corner,
        bias,
        gain.reshape(1, C),
        w_qkv,
        w_proj,
    )

    taken = other_core(given)
    west = shifted(back_east, 1, 0)
    far = shifted(back_corner, 1, 1)
    north = shifted(back_south, 0, 1)
    packed = call(
        table_kernel,
        "table_grads",
        jax.ShapeDtypeStruct((TROWS, 128), BF16),
        [pltpu.VMEM((CHUNKS, GROUPS, 128), F32)],
    )(codes, inverse)

    lats, lons = lax.axis_size("lat"), lax.axis_size("lon")
    ring, cross = peers(("z", "x_lo")), peers(("x_hi", "y"))
    count = len(ring[0])
    w_rows, t_rows = WROWS // 2 // count, TROWS // count
    mine = (kept.astype(F32) + taken.astype(F32)).astype(BF16).reshape(count, w_rows, 128)
    sent = jnp.concatenate([mine, packed.reshape(count, t_rows, 128)], axis=1)
    parts = exchange(sent, ring)
    table_sums = added(parts[:, w_rows:].reshape(count // 2, 2, t_rows, 128))
    weight_sum = added(parts[:, :w_rows])
    table_sums = added(jnp.stack([table_sums, other_half(table_sums)]))
    weight_sum = added(spread(weight_sum, cross))
    both_sums = jnp.concatenate([jnp.stack([weight_sum, weight_sum]), table_sums], axis=1)
    both_sums = jnp.broadcast_to(both_sums[None], (count // 2,) + both_sums.shape)
    got = exchange(both_sums.reshape(count, w_rows + t_rows, 128), ring)
    packed = got[:, w_rows:].reshape(TROWS, 128)
    kept = got[:, :w_rows].reshape(WROWS // 2, 128)
    taken = other_core(kept)

    upper = jnp.concatenate([far, north], axis=1)
    lower = jnp.concatenate([west, back_own], axis=1)
    back = jnp.concatenate([upper, lower], axis=0)
    d_field = (dy_own.astype(F32) + back.astype(F32)).astype(BF16).transpose(2, 0, 1, 3)

    tokens_total = Z * valid_rows.shape[0] * lons * WW
    d_gain, d_wqkv, d_wproj, d_table = call(
        functools.partial(finish_kernel, tokens_total**-0.5, (lons * WW) ** -0.5),
        "unpack",
        (
            jax.ShapeDtypeStruct((1, C), F32),
            jax.ShapeDtypeStruct((C, 3 * C), F32),
            jax.ShapeDtypeStruct((C, C), F32),
            jax.ShapeDtypeStruct((HEADS, TYPES, POS), F32),
        ),
        [pltpu.VMEM((WROWS, 128), BF16)],
        [smem] + [vmem] * 3,
    )(base, kept, taken, packed)
    return d_field, d_gain.reshape(C), d_wqkv, d_wproj, d_table.transpose(1, 0, 2)


def solution(mesh):
    field = P(None, "lat", "lon", None)
    table = P("lat", None, None)
    return jax.shard_map(
        per_device,
        mesh=mesh,
        in_specs=(field, field, P(), P(), P(), table, P(), P()),
        out_specs=(field, P(), P(), P(), table),
        check_vma=False,
    )
```

```python
import functools
import itertools

import jax
import jax.numpy as jnp
from jax import lax
from jax.experimental import pallas as pl
from jax.experimental.pallas import tpu as pltpu
from jax.sharding import PartitionSpec as P

HEADS = 6
Z = 8
WZ = 2
WH = 6
WW = 12
WIN = 144
POS = 3312
C = 192
HD = 32
TYPES = 4
GROUPS = TYPES * HEADS
PAIRS = 12
SPAN = 2 * WW - 1
LANES = 384
CHUNKS = 26
TAIL = SPAN * PAIRS - 256
SCALE = HD**-0.5
NEG = -1e30
WROWS = 1280
TROWS = 640
AHEAD, BEHIND = 2, 1
F32 = jnp.float32
BF16 = jnp.bfloat16


def nn(left, right):
    return lax.dot_general(left, right, (((1,), (0,)), ((), ())), preferred_element_type=F32)


def nt(left, right):
    return lax.dot_general(left, right, (((1,), (1,)), ((), ())), preferred_element_type=F32)


def bias_kernel(base, position, table, bias, inverse, sheet, codes):
    for head in range(HEADS):
        sheet[head * TYPES : (head + 1) * TYPES, :POS] = table[head]
    sheet[:, POS:] = jnp.zeros((GROUPS, CHUNKS * 128 - POS), F32)
    token = lax.broadcasted_iota(jnp.int32, (WIN, WIN), 0)
    col = lax.div(token, PAIRS)
    place = token - col * PAIRS
    row, level = lax.shift_right_logical(place, 1), lax.bitwise_and(place, 1)
    natural = level * (WH * WW) + row * WW + col
    order = jnp.where(lax.broadcasted_iota(jnp.int32, (WIN, WIN), 1) == natural, 1.0, 0.0)
    order = order.astype(BF16)
    entries = position[...]
    digits = []
    for digit in (lax.shift_right_arithmetic(entries, 7), lax.bitwise_and(entries, 127)):
        turned = nt(order, digit.astype(F32).astype(BF16)).astype(BF16)
        digits.append(nt(turned, order))
    whole_index = digits[0] * 128.0 + digits[1]
    pieces = [
        whole_index[(WW - 1 - gap) * PAIRS : (WW - gap) * PAIRS, :PAIRS] for gap in range(WW - 1)
    ]
    pieces.append(whole_index[:PAIRS, :])
    pieces.append(jnp.full((PAIRS, LANES - SPAN * PAIRS), -1.0, F32))
    index = jnp.concatenate(pieces, axis=1).astype(jnp.int32)

    tails = [
        jnp.concatenate(
            [index[place : place + 1, 256 : 256 + TAIL] for place in range(6 * half, 6 * half + 6)]
            + [jnp.full((1, 128 - 6 * TAIL), -1, jnp.int32)],
            axis=1,
        )
        for half in range(2)
    ]

    def lookup(entry):
        entry = jnp.broadcast_to(entry, (GROUPS, 128))
        high = lax.shift_right_arithmetic(entry, 7)
        low = lax.bitwise_and(entry, 127)
        found = jnp.zeros((GROUPS, 128), F32)
        for chunk in range(CHUNKS):
            source = sheet[:, chunk * 128 : (chunk + 1) * 128]
            found = jnp.where(high == chunk, jnp.take_along_axis(source, low, axis=1), found)
        return found

    last = [lookup(tail) for tail in tails]
    for place in range(PAIRS):
        parts = [lookup(index[place : place + 1, col * 128 : (col + 1) * 128]) for col in range(2)]
        turn = place % 6 * TAIL
        tail = last[place // 6]
        parts.append(tail if turn == 0 else pltpu.roll(tail, 128 - turn, 1))
        row = jnp.concatenate(parts, axis=1)
        moved = pltpu.roll(row, PAIRS, 1)
        for col in range(3):
            at = slice(col * 128, (col + 1) * 128)
            codes[col, pl.ds(place, GROUPS, stride=24), :] = row[:, at]
            codes[col, pl.ds(PAIRS + place, GROUPS, stride=24), :] = moved[:, at]

    first = base[0]
    lat_total = base.shape[0] - 2

    def places(shape, axis):
        token = lax.broadcasted_iota(jnp.int32, shape, axis)
        place = lax.rem(token, PAIRS)
        row, level = lax.shift_right_logical(place, 1), lax.bitwise_and(place, 1)
        return row, level, (first + row >= lat_total - WH // 2).astype(jnp.int32)

    key_row, key_level, key_late = places((WIN, 1), 0)
    _, query_level, query_late = places((1, WIN), 1)
    good = jnp.zeros((WIN, 1), jnp.int32)
    for row in range(WH):
        valid = base[2 + lax.rem(first + row + WH // 2, lat_total)]
        good = jnp.where(key_row == row, valid, good)
    rows_allowed = (key_late == query_late) & (good > 0)
    top_allowed = rows_allowed & (key_level == query_level)
    for window in range(TYPES):
        allowed = top_allowed if window == TYPES - 1 else rows_allowed
        for head in range(HEADS):
            group = head * TYPES + window
            block = jnp.concatenate(
                [codes[col, group * 24 : (group + 1) * 24, :] for col in range(3)], axis=1
            )
            pieces = []
            for step in range(WW // 2):
                turned = pltpu.roll(block, LANES - (132 - 24 * step), 1)
                pieces.append(turned[:, :WIN])
            full = jnp.concatenate(pieces, axis=0)
            bias[group] = jnp.where(allowed, full, NEG)
    total = jnp.zeros((64, 128), F32)
    lane = lax.broadcasted_iota(jnp.int32, (32, 128), 1).astype(F32)
    tall = lax.broadcasted_iota(jnp.int32, (32, 128), 0)
    deep = lax.broadcasted_iota(jnp.int32, (128, 128), 0)
    rows = [index[place : place + 1, at : at + 128] for place in range(PAIRS) for at in (0, 128)]
    for chunk, entry in enumerate(rows + tails):
        high = lax.shift_right_arithmetic(entry, 7)
        low = lax.bitwise_and(entry, 127)
        hit = high == tall
        left = jnp.concatenate([jnp.where(hit, float(chunk), 0.0), jnp.where(hit, lane, 0.0)], axis=0)
        right = jnp.where(deep == low, 1.0, 0.0).astype(BF16)
        total = total + nt(left.astype(BF16), right)
    inverse[...] = total.astype(jnp.int32)


def window_kernel(
    base,
    own,
    east,
    south,
    corner,
    bias,
    gain,
    wq,
    wp,
    back_own,
    back_east,
    back_south,
    back_corner,
    codes,
    kept,
    given,
    natural,
    windows,
    weights,
):
    half_r, half_c = WH // 2, WW // 2
    for col in range(WW):
        for row in range(WH):
            if row < half_r:
                source = own if col < half_c else east
            else:
                source = south if col < half_c else corner
            tile = source[row % half_r, col % half_c].astype(F32)
            at = (col * WH + row) * Z
            for part in range(3):
                natural[part, at : at + Z, :] = tile[:, part * 128 : (part + 1) * 128]
    for part in range(3):
        for window in range(TYPES):
            for level in range(WZ):
                source = natural[part, pl.ds((WZ * window + level + 1) % Z, 72, stride=Z), :]
                windows[part, pl.ds(window * WIN + level, 72, stride=WZ), :] = source

    tokens = jnp.concatenate([windows[0], windows[1][:, :64]], axis=1)
    grads_all = jnp.concatenate([windows[1][:, 64:], windows[2]], axis=1).astype(BF16)
    average = jnp.mean(tokens, axis=1, keepdims=True)
    centred = tokens - average
    inv_std_all = lax.rsqrt(jnp.mean(centred * centred, axis=1, keepdims=True) + 1e-5)
    normed_all = centred * inv_std_all
    gains = gain[...]
    hidden_all = (normed_all * gains).astype(BF16)
    wq_t = wq[...].astype(F32).T.astype(BF16)
    key_value = nn(hidden_all, wq[:, C:]).astype(BF16)

    totals = [None, None, None]

    def prepare(window):
        span = slice(window * WIN, (window + 1) * WIN)
        state = {"span": span, "hidden": hidden_all[span], "grads": grads_all[span]}
        state["keys"], state["values"] = key_value[span, :C], key_value[span, C:]
        state["qkv_t"] = nt(wq_t, state["hidden"]).astype(BF16)
        state["datt_t"] = nt(wp[...], state["grads"]).astype(BF16)
        for name in ("att", "dq", "dk", "dv"):
            state[name] = []
        return state

    def features(state, head):
        part = [state["qkv_t"][at + head * HD : at + (head + 1) * HD] for at in (0, C, 2 * C)]
        return part + [state["datt_t"][head * HD : (head + 1) * HD]]

    def products(state, head):
        q_t, _, _, a_t = features(state, head)
        scores = nn(state["keys"][:, head * HD : (head + 1) * HD], q_t)
        d_probs = nn(state["values"][:, head * HD : (head + 1) * HD], a_t)
        return scores, d_probs

    def softmax(window, head, scores, d_probs):
        scores = scores * SCALE + bias[head * TYPES + window]
        raised = jnp.exp(scores - jnp.max(scores, axis=0, keepdims=True))
        probs = raised * (1.0 / jnp.sum(raised, axis=0, keepdims=True))
        d_scores = probs * (d_probs - jnp.sum(d_probs * probs, axis=0, keepdims=True))
        return probs.astype(BF16), d_scores

    def gradients(state, window, head, probs_b, d_scores):
        q_t, k_t, v_t, a_t = features(state, head)
        group = head * TYPES + window
        d_scores_b = (d_scores * SCALE).astype(BF16)
        state["att"].append(nn(v_t, probs_b).astype(BF16))
        state["dq"].append(nn(k_t, d_scores_b).astype(BF16))
        state["dk"].append(nt(q_t, d_scores_b).astype(BF16))
        state["dv"].append(nt(a_t, probs_b).astype(BF16))
        folded = None
        for part in range(WW // 2):
            rows = d_scores[part * 24 : (part + 1) * 24]
            rows = jnp.concatenate([rows, jnp.zeros((24, LANES - WIN), F32)], axis=1)
            folded = rows if part == 0 else pltpu.roll(folded, 24, 1) + rows
        folded = pltpu.roll(folded, PAIRS, 1)
        for col in range(3):
            codes[col, group * 24 : (group + 1) * 24, :] = folded[:, col * 128 : (col + 1) * 128]

    def close(state):
        span, hidden, grads = state["span"], state["hidden"], state["grads"]
        normed, inv_std = normed_all[span], inv_std_all[span]
        att_t = jnp.concatenate(state["att"], axis=0)
        dqkv_t = jnp.concatenate(state["dq"] + state["dk"] + state["dv"], axis=0)
        d_hidden = nn(wq[...], dqkv_t).T
        parts = (
            nn(dqkv_t, hidden),
            nn(att_t, grads),
            jnp.sum(d_hidden * normed, axis=0, keepdims=True),
        )
        for at, part in enumerate(parts):
            totals[at] = part if totals[at] is None else totals[at] + part
        d_norm = d_hidden * gains
        branch = inv_std * (
            d_norm
            - jnp.mean(d_norm, axis=1, keepdims=True)
            - normed * jnp.mean(d_norm * normed, axis=1, keepdims=True)
        )
        windows[0, span, :] = branch[:, :128]
        windows[1, span, :64] = branch[:, 128:]

    states, first, second = {}, {}, {}
    for step in range(GROUPS + AHEAD + BEHIND):
        if step < GROUPS:
            window, head = divmod(step, HEADS)
            if head == 0:
                states[window] = prepare(window)
            first[step] = products(states[window], head)
        at = step - AHEAD
        if 0 <= at < GROUPS:
            window, head = divmod(at, HEADS)
            second[at] = softmax(window, head, *first.pop(at))
        at = step - AHEAD - BEHIND
        if at >= 0:
            window, head = divmod(at, HEADS)
            gradients(states[window], window, head, *second.pop(at))
            if head == HEADS - 1:
                close(states.pop(window))
    dw, dp, dg = totals

    for part in range(2):
        for window in range(TYPES):
            for level in range(WZ):
                source = windows[part, pl.ds(window * WIN + level, 72, stride=WZ), :]
                natural[part, pl.ds((WZ * window + level + 1) % Z, 72, stride=Z), :] = source
    for col in range(WW):
        for row in range(WH):
            at = (col * WH + row) * Z
            tile = jnp.concatenate(
                [natural[0, at : at + Z, :], natural[1, at : at + Z, :64]], axis=1
            )
            if row < half_r:
                target = back_own if col < half_c else back_east
            else:
                target = back_south if col < half_c else back_corner
            target[row % half_r, col % half_c] = tile.astype(BF16)

    weights[0:576, :] = dw[:, :128].astype(BF16)
    weights[576:864, :] = jnp.concatenate([dw[:288, 128:], dw[288:, 128:]], axis=1).astype(BF16)
    weights[864:1056, :] = dp[:, :128].astype(BF16)
    weights[1056:1152, :] = jnp.concatenate([dp[:96, 128:], dp[96:, 128:]], axis=1).astype(BF16)
    wide = jnp.concatenate([dg, jnp.zeros((1, 64), F32)], axis=1)
    last = jnp.concatenate([wide[:, :128], wide[:, 128:], jnp.zeros((126, 128), F32)], axis=0)
    weights[1152:1280, :] = last.astype(BF16)
    core = base[1]
    half = WROWS // 2
    kept[...] = weights[pl.ds(pl.multiple_of(core * half, half), half), :]
    given[...] = weights[pl.ds(pl.multiple_of((1 - core) * half, half), half), :]


def table_kernel(codes, inverse, packed, rows):
    lane = lax.broadcasted_iota(jnp.int32, (GROUPS, 128), 1)
    tails = [jnp.zeros((GROUPS, 128), F32), jnp.zeros((GROUPS, 128), F32)]
    for place in range(PAIRS):
        above = jnp.concatenate(
            [codes[col, pl.ds(place, GROUPS, stride=24), :] for col in range(3)], axis=1
        )
        below = jnp.concatenate(
            [codes[col, pl.ds(PAIRS + place, GROUPS, stride=24), :] for col in range(3)], axis=1
        )
        both = above + pltpu.roll(below, LANES - PAIRS, 1)
        rows[2 * place] = both[:, :128]
        rows[2 * place + 1] = both[:, 128:256]
        turn = place % 6 * TAIL
        tail = both[:, 256:]
        tail = tail if turn == 0 else pltpu.roll(tail, turn, 1)
        inside = (lane >= turn) & (lane < turn + TAIL)
        tails[place // 6] = jnp.where(inside, tail, tails[place // 6])
    rows[2 * PAIRS] = tails[0]
    rows[2 * PAIRS + 1] = tails[1]
    for chunk in range(CHUNKS):
        source = jnp.broadcast_to(inverse[chunk : chunk + 1, :], (GROUPS, 128))
        low = jnp.broadcast_to(inverse[32 + chunk : 33 + chunk, :], (GROUPS, 128))
        found = jnp.zeros((GROUPS, 128), F32)
        for at in range(CHUNKS):
            found = jnp.where(source == at, jnp.take_along_axis(rows[at], low, axis=1), found)
        packed[chunk * GROUPS : (chunk + 1) * GROUPS, :] = found.astype(BF16)
    packed[CHUNKS * GROUPS :, :] = jnp.zeros((TROWS - CHUNKS * GROUPS, 128), BF16)


def finish_kernel(
    grad_scale, table_scale, base, kept, taken, packed_t, d_gain, d_wqkv, d_wproj, d_table, weights
):
    core = base[1]
    half = WROWS // 2
    weights[pl.ds(pl.multiple_of(core * half, half), half), :] = kept[...]
    weights[pl.ds(pl.multiple_of((1 - core) * half, half), half), :] = taken[...]
    scaled = weights[...].astype(F32) * grad_scale
    side = scaled[576:864]
    right = jnp.concatenate([side[:, :64], side[:, 64:]], axis=0)
    d_wqkv[...] = jnp.concatenate([scaled[:576], right], axis=1).T
    side = scaled[1056:1152]
    right = jnp.concatenate([side[:, :64], side[:, 64:]], axis=0)
    d_wproj[...] = jnp.concatenate([scaled[864:1056], right], axis=1)
    d_gain[...] = jnp.concatenate([scaled[1152:1153], scaled[1153:1154, :64]], axis=1)
    for chunk in range(CHUNKS):
        part = packed_t[chunk * 24 : (chunk + 1) * 24, :].astype(F32) * table_scale
        width = min(128, POS - chunk * 128)
        for head in range(HEADS):
            d_table[head, :, chunk * 128 : chunk * 128 + width] = part[
                head * TYPES : (head + 1) * TYPES, :width
            ]


def shifted(value, steps_lon, steps_lat):
    lons, lats = lax.axis_size("lon"), lax.axis_size("lat")
    pairs = [
        (i * lats + j, (i + steps_lon) % lons * lats + (j + steps_lat) % lats)
        for i in range(lons)
        for j in range(lats)
    ]
    return lax.ppermute(value, ("lon", "lat"), pairs)


def other_core(value):
    count = lax.axis_size("lat")
    return lax.ppermute(value, "lat", [(i, i ^ 1) for i in range(count)])


def other_half(value):
    count = lax.axis_size("lon")
    return lax.ppermute(value, "lon", [(i, i ^ 1) for i in range(count)])


def peers(names):
    lons, lats = lax.axis_size("lon"), lax.axis_size("lat")
    sizes = {"z": lons // 2, "x_hi": 2, "x_lo": 2, "y": lats // 4, "core": 2}
    others = [name for name in sizes if name not in names]

    def places(wanted):
        return itertools.product(*[range(sizes[name]) for name in wanted])

    def device(at):
        lon = at["z"] * sizes["x_hi"] + at["x_hi"]
        lat = (at["x_lo"] * sizes["y"] + at["y"]) * sizes["core"] + at["core"]
        return lon * lats + lat

    return [
        [device(dict(zip(others, fixed)) | dict(zip(names, place))) for place in places(names)]
        for fixed in places(others)
    ]


def exchange(value, groups):
    return lax.all_to_all(value, ("lon", "lat"), 0, 0, axis_index_groups=groups)


def added(pieces):
    return jnp.sum(pieces.astype(F32), axis=0).astype(BF16)


def spread(piece, groups):
    return exchange(jnp.broadcast_to(piece[None], (len(groups[0]),) + piece.shape), groups)


def call(kernel, name, out_shape, scratch=(), in_specs=None, limit=16, micros=2):
    extra = {} if in_specs is None else {"in_specs": in_specs}
    return pl.pallas_call(
        kernel,
        out_shape=out_shape,
        scratch_shapes=list(scratch),
        compiler_params=pltpu.CompilerParams(vmem_limit_bytes=limit * 2**20),
        name=name,
        cost_estimate=pl.CostEstimate(
            flops=micros * 10**9, bytes_accessed=micros * 3 * 10**6, transcendentals=0
        ),
        **extra,
    )


def per_device(x_field, cotangent, gain, w_qkv, w_proj, bias_table, position_index, valid_rows):
    half_r, half_c = WH // 2, WW // 2
    x_own = x_field.transpose(1, 2, 0, 3)
    dy_own = cotangent.transpose(1, 2, 0, 3)

    def both(rows, cols):
        return jnp.concatenate([x_own[rows, cols], dy_own[rows, cols]], axis=3)

    top, bottom = slice(0, half_r), slice(half_r, WH)
    left, right = slice(0, half_c), slice(half_c, WW)
    east = shifted(both(bottom, left), -1, 0)
    corner = shifted(both(top, left), -1, -1)
    south = shifted(both(top, right), 0, -1)

    lat = lax.axis_index("lat").astype(jnp.int32)
    base = jnp.concatenate([jnp.stack([lat * WH, lat % 2]), valid_rows])
    vmem, smem = pl.BlockSpec(memory_space=pltpu.VMEM), pl.BlockSpec(memory_space=pltpu.SMEM)
    quarter = jax.ShapeDtypeStruct((half_r, half_c, Z, C), BF16)
    bias, inverse = call(
        bias_kernel,
        "bias_lookup",
        (
            jax.ShapeDtypeStruct((GROUPS, WIN, WIN), F32),
            jax.ShapeDtypeStruct((64, 128), jnp.int32),
        ),
        [
            pltpu.VMEM((GROUPS, CHUNKS * 128), F32),
            pltpu.VMEM((3, GROUPS * 24, 128), F32),
        ],
        [smem, vmem, vmem],
        micros=6,
    )(base, position_index, bias_table.transpose(1, 0, 2))

    half_w = jax.ShapeDtypeStruct((WROWS // 2, 128), BF16)
    back_own, back_east, back_south, back_corner, codes, kept, given = call(
        window_kernel,
        "window_grads",
        (
            quarter,
            quarter,
            quarter,
            quarter,
            jax.ShapeDtypeStruct((3, GROUPS * 24, 128), F32),
            half_w,
            half_w,
        ),
        [
            pltpu.VMEM((3, 576, 128), F32),
            pltpu.VMEM((3, 576, 128), F32),
            pltpu.VMEM((WROWS, 128), BF16),
        ],
        [smem] + [vmem] * 8,
        limit=24,
        micros=7,
    )(
        base,
        both(bottom, right),
        east,
        south,
        corner,
        bias,
        gain.reshape(1, C),
        w_qkv,
        w_proj,
    )

    taken = other_core(given)
    west = shifted(back_east, 1, 0)
    far = shifted(back_corner, 1, 1)
    north = shifted(back_south, 0, 1)
    packed = call(
        table_kernel,
        "table_grads",
        jax.ShapeDtypeStruct((TROWS, 128), BF16),
        [pltpu.VMEM((CHUNKS, GROUPS, 128), F32)],
    )(codes, inverse)

    lats, lons = lax.axis_size("lat"), lax.axis_size("lon")
    ring, cross = peers(("z", "y")), peers(("x_hi", "x_lo"))
    count = len(ring[0])
    w_rows, t_rows = WROWS // 2 // count, TROWS // count
    mine = (kept.astype(F32) + taken.astype(F32)).astype(BF16).reshape(count, w_rows, 128)
    sent = jnp.concatenate([mine, packed.reshape(count, t_rows, 128)], axis=1)
    parts = exchange(sent, ring)
    table_sums = added(parts[:, w_rows:].reshape(count // 4, 4, t_rows, 128))
    weight_sum = added(parts[:, :w_rows])
    table_sums = added(jnp.stack([table_sums, other_half(table_sums)]))
    weight_sum = added(spread(weight_sum, cross))
    both_sums = jnp.concatenate([jnp.stack([weight_sum] * 4), table_sums], axis=1)
    both_sums = jnp.broadcast_to(both_sums[None], (count // 4,) + both_sums.shape)
    got = exchange(both_sums.reshape(count, w_rows + t_rows, 128), ring)
    packed = got[:, w_rows:].reshape(TROWS, 128)
    kept = got[:, :w_rows].reshape(WROWS // 2, 128)
    taken = other_core(kept)

    upper = jnp.concatenate([far, north], axis=1)
    lower = jnp.concatenate([west, back_own], axis=1)
    back = jnp.concatenate([upper, lower], axis=0)
    d_field = (dy_own.astype(F32) + back.astype(F32)).astype(BF16).transpose(2, 0, 1, 3)

    tokens_total = Z * valid_rows.shape[0] * lons * WW
    d_gain, d_wqkv, d_wproj, d_table = call(
        functools.partial(finish_kernel, tokens_total**-0.5, (lons * WW) ** -0.5),
        "unpack",
        (
            jax.ShapeDtypeStruct((1, C), F32),
            jax.ShapeDtypeStruct((C, 3 * C), F32),
            jax.ShapeDtypeStruct((C, C), F32),
            jax.ShapeDtypeStruct((HEADS, TYPES, POS), F32),
        ),
        [pltpu.VMEM((WROWS, 128), BF16)],
        [smem] + [vmem] * 3,
    )(base, kept, taken, packed)
    return d_field, d_gain.reshape(C), d_wqkv, d_wproj, d_table.transpose(1, 0, 2)


def solution(mesh):
    field = P(None, "lat", "lon", None)
    table = P("lat", None, None)
    return jax.shard_map(
        per_device,
        mesh=mesh,
        in_specs=(field, field, P(), P(), P(), table, P(), P()),
        out_specs=(field, P(), P(), P(), table),
        check_vma=False,
    )
```

```python
import functools
import itertools

import jax
import jax.numpy as jnp
from jax import lax
from jax.experimental import pallas as pl
from jax.experimental.pallas import tpu as pltpu
from jax.sharding import PartitionSpec as P

HEADS = 6
Z = 8
WZ = 2
WH = 6
WW = 12
WIN = 144
POS = 3312
C = 192
HD = 32
TYPES = 4
GROUPS = TYPES * HEADS
PAIRS = 12
SPAN = 2 * WW - 1
LANES = 384
CHUNKS = 26
TAIL = SPAN * PAIRS - 256
SCALE = HD**-0.5
NEG = -1e30
WROWS = 1280
TROWS = 640
AHEAD, BEHIND = 2, 1
F32 = jnp.float32
BF16 = jnp.bfloat16


def nn(left, right):
    return lax.dot_general(left, right, (((1,), (0,)), ((), ())), preferred_element_type=F32)


def nt(left, right):
    return lax.dot_general(left, right, (((1,), (1,)), ((), ())), preferred_element_type=F32)


def bias_kernel(base, position, table, bias, inverse, sheet, codes):
    for head in range(HEADS):
        sheet[head * TYPES : (head + 1) * TYPES, :POS] = table[head]
    sheet[:, POS:] = jnp.zeros((GROUPS, CHUNKS * 128 - POS), F32)
    token = lax.broadcasted_iota(jnp.int32, (WIN, WIN), 0)
    col = lax.div(token, PAIRS)
    place = token - col * PAIRS
    row, level = lax.shift_right_logical(place, 1), lax.bitwise_and(place, 1)
    natural = level * (WH * WW) + row * WW + col
    order = jnp.where(lax.broadcasted_iota(jnp.int32, (WIN, WIN), 1) == natural, 1.0, 0.0)
    order = order.astype(BF16)
    entries = position[...]
    digits = []
    for digit in (lax.shift_right_arithmetic(entries, 7), lax.bitwise_and(entries, 127)):
        turned = nt(order, digit.astype(F32).astype(BF16)).astype(BF16)
        digits.append(nt(turned, order))
    whole_index = digits[0] * 128.0 + digits[1]
    pieces = [
        whole_index[(WW - 1 - gap) * PAIRS : (WW - gap) * PAIRS, :PAIRS] for gap in range(WW - 1)
    ]
    pieces.append(whole_index[:PAIRS, :])
    pieces.append(jnp.full((PAIRS, LANES - SPAN * PAIRS), -1.0, F32))
    index = jnp.concatenate(pieces, axis=1).astype(jnp.int32)

    tails = [
        jnp.concatenate(
            [index[place : place + 1, 256 : 256 + TAIL] for place in range(6 * half, 6 * half + 6)]
            + [jnp.full((1, 128 - 6 * TAIL), -1, jnp.int32)],
            axis=1,
        )
        for half in range(2)
    ]

    def lookup(entry):
        entry = jnp.broadcast_to(entry, (GROUPS, 128))
        high = lax.shift_right_arithmetic(entry, 7)
        low = lax.bitwise_and(entry, 127)
        found = jnp.zeros((GROUPS, 128), F32)
        for chunk in range(CHUNKS):
            source = sheet[:, chunk * 128 : (chunk + 1) * 128]
            found = jnp.where(high == chunk, jnp.take_along_axis(source, low, axis=1), found)
        return found

    last = [lookup(tail) for tail in tails]
    for place in range(PAIRS):
        parts = [lookup(index[place : place + 1, col * 128 : (col + 1) * 128]) for col in range(2)]
        turn = place % 6 * TAIL
        tail = last[place // 6]
        parts.append(tail if turn == 0 else pltpu.roll(tail, 128 - turn, 1))
        row = jnp.concatenate(parts, axis=1)
        moved = pltpu.roll(row, PAIRS, 1)
        for col in range(3):
            at = slice(col * 128, (col + 1) * 128)
            codes[col, pl.ds(place, GROUPS, stride=24), :] = row[:, at]
            codes[col, pl.ds(PAIRS + place, GROUPS, stride=24), :] = moved[:, at]

    first = base[0]
    lat_total = base.shape[0] - 2

    def places(shape, axis):
        token = lax.broadcasted_iota(jnp.int32, shape, axis)
        place = lax.rem(token, PAIRS)
        row, level = lax.shift_right_logical(place, 1), lax.bitwise_and(place, 1)
        return row, level, (first + row >= lat_total - WH // 2).astype(jnp.int32)

    key_row, key_level, key_late = places((WIN, 1), 0)
    _, query_level, query_late = places((1, WIN), 1)
    good = jnp.zeros((WIN, 1), jnp.int32)
    for row in range(WH):
        valid = base[2 + lax.rem(first + row + WH // 2, lat_total)]
        good = jnp.where(key_row == row, valid, good)
    rows_allowed = (key_late == query_late) & (good > 0)
    top_allowed = rows_allowed & (key_level == query_level)
    for window in range(TYPES):
        allowed = top_allowed if window == TYPES - 1 else rows_allowed
        for head in range(HEADS):
            group = head * TYPES + window
            block = jnp.concatenate(
                [codes[col, group * 24 : (group + 1) * 24, :] for col in range(3)], axis=1
            )
            pieces = []
            for step in range(WW // 2):
                turned = pltpu.roll(block, LANES - (132 - 24 * step), 1)
                pieces.append(turned[:, :WIN])
            full = jnp.concatenate(pieces, axis=0)
            bias[group] = jnp.where(allowed, full, NEG)
    total = jnp.zeros((64, 128), F32)
    lane = lax.broadcasted_iota(jnp.int32, (32, 128), 1).astype(F32)
    tall = lax.broadcasted_iota(jnp.int32, (32, 128), 0)
    deep = lax.broadcasted_iota(jnp.int32, (128, 128), 0)
    rows = [index[place : place + 1, at : at + 128] for place in range(PAIRS) for at in (0, 128)]
    for chunk, entry in enumerate(rows + tails):
        high = lax.shift_right_arithmetic(entry, 7)
        low = lax.bitwise_and(entry, 127)
        hit = high == tall
        left = jnp.concatenate([jnp.where(hit, float(chunk), 0.0), jnp.where(hit, lane, 0.0)], axis=0)
        right = jnp.where(deep == low, 1.0, 0.0).astype(BF16)
        total = total + nt(left.astype(BF16), right)
    inverse[...] = total.astype(jnp.int32)


def window_kernel(
    base,
    own,
    east,
    south,
    corner,
    bias,
    gain,
    wq,
    wp,
    back_own,
    back_east,
    back_south,
    back_corner,
    codes,
    kept,
    given,
    natural,
    windows,
    weights,
):
    half_r, half_c = WH // 2, WW // 2
    for col in range(WW):
        for row in range(WH):
            if row < half_r:
                source = own if col < half_c else east
            else:
                source = south if col < half_c else corner
            tile = source[row % half_r, col % half_c].astype(F32)
            at = (col * WH + row) * Z
            for part in range(3):
                natural[part, at : at + Z, :] = tile[:, part * 128 : (part + 1) * 128]
    for part in range(3):
        for window in range(TYPES):
            for level in range(WZ):
                source = natural[part, pl.ds((WZ * window + level + 1) % Z, 72, stride=Z), :]
                windows[part, pl.ds(window * WIN + level, 72, stride=WZ), :] = source

    tokens = jnp.concatenate([windows[0], windows[1][:, :64]], axis=1)
    grads_all = jnp.concatenate([windows[1][:, 64:], windows[2]], axis=1).astype(BF16)
    average = jnp.mean(tokens, axis=1, keepdims=True)
    centred = tokens - average
    inv_std_all = lax.rsqrt(jnp.mean(centred * centred, axis=1, keepdims=True) + 1e-5)
    normed_all = centred * inv_std_all
    gains = gain[...]
    hidden_all = (normed_all * gains).astype(BF16)
    wq_t = wq[...].astype(F32).T.astype(BF16)
    key_value = nn(hidden_all, wq[:, C:]).astype(BF16)

    totals = [None, None, None]

    def prepare(window):
        span = slice(window * WIN, (window + 1) * WIN)
        state = {"span": span, "hidden": hidden_all[span], "grads": grads_all[span]}
        state["keys"], state["values"] = key_value[span, :C], key_value[span, C:]
        state["qkv_t"] = nt(wq_t, state["hidden"]).astype(BF16)
        state["datt_t"] = nt(wp[...], state["grads"]).astype(BF16)
        for name in ("att", "dq", "dk", "dv"):
            state[name] = []
        return state

    def features(state, head):
        part = [state["qkv_t"][at + head * HD : at + (head + 1) * HD] for at in (0, C, 2 * C)]
        return part + [state["datt_t"][head * HD : (head + 1) * HD]]

    def products(state, head):
        q_t, _, _, a_t = features(state, head)
        scores = nn(state["keys"][:, head * HD : (head + 1) * HD], q_t)
        d_probs = nn(state["values"][:, head * HD : (head + 1) * HD], a_t)
        return scores, d_probs

    def softmax(window, head, scores, d_probs):
        scores = scores * SCALE + bias[head * TYPES + window]
        raised = jnp.exp(scores - jnp.max(scores, axis=0, keepdims=True))
        probs = raised * (1.0 / jnp.sum(raised, axis=0, keepdims=True))
        d_scores = probs * (d_probs - jnp.sum(d_probs * probs, axis=0, keepdims=True))
        return probs.astype(BF16), d_scores

    def gradients(state, window, head, probs_b, d_scores):
        q_t, k_t, v_t, a_t = features(state, head)
        group = head * TYPES + window
        d_scores_b = (d_scores * SCALE).astype(BF16)
        state["att"].append(nn(v_t, probs_b).astype(BF16))
        state["dq"].append(nn(k_t, d_scores_b).astype(BF16))
        state["dk"].append(nt(q_t, d_scores_b).astype(BF16))
        state["dv"].append(nt(a_t, probs_b).astype(BF16))
        folded = None
        for part in range(WW // 2):
            rows = d_scores[part * 24 : (part + 1) * 24]
            rows = jnp.concatenate([rows, jnp.zeros((24, LANES - WIN), F32)], axis=1)
            folded = rows if part == 0 else pltpu.roll(folded, 24, 1) + rows
        folded = pltpu.roll(folded, PAIRS, 1)
        for col in range(3):
            codes[col, group * 24 : (group + 1) * 24, :] = folded[:, col * 128 : (col + 1) * 128]

    def close(state):
        span, hidden, grads = state["span"], state["hidden"], state["grads"]
        normed, inv_std = normed_all[span], inv_std_all[span]
        att_t = jnp.concatenate(state["att"], axis=0)
        dqkv_t = jnp.concatenate(state["dq"] + state["dk"] + state["dv"], axis=0)
        d_hidden = nn(wq[...], dqkv_t).T
        parts = (
            nn(dqkv_t, hidden),
            nn(att_t, grads),
            jnp.sum(d_hidden * normed, axis=0, keepdims=True),
        )
        for at, part in enumerate(parts):
            totals[at] = part if totals[at] is None else totals[at] + part
        d_norm = d_hidden * gains
        branch = inv_std * (
            d_norm
            - jnp.mean(d_norm, axis=1, keepdims=True)
            - normed * jnp.mean(d_norm * normed, axis=1, keepdims=True)
        )
        windows[0, span, :] = branch[:, :128]
        windows[1, span, :64] = branch[:, 128:]

    states, first, second = {}, {}, {}
    for step in range(GROUPS + AHEAD + BEHIND):
        if step < GROUPS:
            window, head = divmod(step, HEADS)
            if head == 0:
                states[window] = prepare(window)
            first[step] = products(states[window], head)
        at = step - AHEAD
        if 0 <= at < GROUPS:
            window, head = divmod(at, HEADS)
            second[at] = softmax(window, head, *first.pop(at))
        at = step - AHEAD - BEHIND
        if at >= 0:
            window, head = divmod(at, HEADS)
            gradients(states[window], window, head, *second.pop(at))
            if head == HEADS - 1:
                close(states.pop(window))
    dw, dp, dg = totals

    for part in range(2):
        for window in range(TYPES):
            for level in range(WZ):
                source = windows[part, pl.ds(window * WIN + level, 72, stride=WZ), :]
                natural[part, pl.ds((WZ * window + level + 1) % Z, 72, stride=Z), :] = source
    for col in range(WW):
        for row in range(WH):
            at = (col * WH + row) * Z
            tile = jnp.concatenate(
                [natural[0, at : at + Z, :], natural[1, at : at + Z, :64]], axis=1
            )
            if row < half_r:
                target = back_own if col < half_c else back_east
            else:
                target = back_south if col < half_c else back_corner
            target[row % half_r, col % half_c] = tile.astype(BF16)

    weights[0:576, :] = dw[:, :128].astype(BF16)
    weights[576:864, :] = jnp.concatenate([dw[:288, 128:], dw[288:, 128:]], axis=1).astype(BF16)
    weights[864:1056, :] = dp[:, :128].astype(BF16)
    weights[1056:1152, :] = jnp.concatenate([dp[:96, 128:], dp[96:, 128:]], axis=1).astype(BF16)
    wide = jnp.concatenate([dg, jnp.zeros((1, 64), F32)], axis=1)
    last = jnp.concatenate([wide[:, :128], wide[:, 128:], jnp.zeros((126, 128), F32)], axis=0)
    weights[1152:1280, :] = last.astype(BF16)
    core = base[1]
    half = WROWS // 2
    kept[...] = weights[pl.ds(pl.multiple_of(core * half, half), half), :]
    given[...] = weights[pl.ds(pl.multiple_of((1 - core) * half, half), half), :]


def table_kernel(codes, inverse, packed, rows):
    lane = lax.broadcasted_iota(jnp.int32, (GROUPS, 128), 1)
    tails = [jnp.zeros((GROUPS, 128), F32), jnp.zeros((GROUPS, 128), F32)]
    for place in range(PAIRS):
        above = jnp.concatenate(
            [codes[col, pl.ds(place, GROUPS, stride=24), :] for col in range(3)], axis=1
        )
        below = jnp.concatenate(
            [codes[col, pl.ds(PAIRS + place, GROUPS, stride=24), :] for col in range(3)], axis=1
        )
        both = above + pltpu.roll(below, LANES - PAIRS, 1)
        rows[2 * place] = both[:, :128]
        rows[2 * place + 1] = both[:, 128:256]
        turn = place % 6 * TAIL
        tail = both[:, 256:]
        tail = tail if turn == 0 else pltpu.roll(tail, turn, 1)
        inside = (lane >= turn) & (lane < turn + TAIL)
        tails[place // 6] = jnp.where(inside, tail, tails[place // 6])
    rows[2 * PAIRS] = tails[0]
    rows[2 * PAIRS + 1] = tails[1]
    for chunk in range(CHUNKS):
        source = jnp.broadcast_to(inverse[chunk : chunk + 1, :], (GROUPS, 128))
        low = jnp.broadcast_to(inverse[32 + chunk : 33 + chunk, :], (GROUPS, 128))
        found = jnp.zeros((GROUPS, 128), F32)
        for at in range(CHUNKS):
            found = jnp.where(source == at, jnp.take_along_axis(rows[at], low, axis=1), found)
        packed[chunk * GROUPS : (chunk + 1) * GROUPS, :] = found.astype(BF16)
    packed[CHUNKS * GROUPS :, :] = jnp.zeros((TROWS - CHUNKS * GROUPS, 128), BF16)


def finish_kernel(
    grad_scale, table_scale, base, kept, taken, packed_t, d_gain, d_wqkv, d_wproj, d_table, weights
):
    core = base[1]
    half = WROWS // 2
    weights[pl.ds(pl.multiple_of(core * half, half), half), :] = kept[...]
    weights[pl.ds(pl.multiple_of((1 - core) * half, half), half), :] = taken[...]
    scaled = weights[...].astype(F32) * grad_scale
    side = scaled[576:864]
    right = jnp.concatenate([side[:, :64], side[:, 64:]], axis=0)
    d_wqkv[...] = jnp.concatenate([scaled[:576], right], axis=1).T
    side = scaled[1056:1152]
    right = jnp.concatenate([side[:, :64], side[:, 64:]], axis=0)
    d_wproj[...] = jnp.concatenate([scaled[864:1056], right], axis=1)
    d_gain[...] = jnp.concatenate([scaled[1152:1153], scaled[1153:1154, :64]], axis=1)
    for chunk in range(CHUNKS):
        part = packed_t[chunk * 24 : (chunk + 1) * 24, :].astype(F32) * table_scale
        width = min(128, POS - chunk * 128)
        for head in range(HEADS):
            d_table[head, :, chunk * 128 : chunk * 128 + width] = part[
                head * TYPES : (head + 1) * TYPES, :width
            ]


def shifted(value, steps_lon, steps_lat):
    lons, lats = lax.axis_size("lon"), lax.axis_size("lat")
    pairs = [
        (i * lats + j, (i + steps_lon) % lons * lats + (j + steps_lat) % lats)
        for i in range(lons)
        for j in range(lats)
    ]
    return lax.ppermute(value, ("lon", "lat"), pairs)


def other_core(value):
    count = lax.axis_size("lat")
    return lax.ppermute(value, "lat", [(i, i ^ 1) for i in range(count)])


def other_half(value):
    count = lax.axis_size("lon")
    return lax.ppermute(value, "lon", [(i, i ^ 1) for i in range(count)])


def peers(names):
    lons, lats = lax.axis_size("lon"), lax.axis_size("lat")
    sizes = {"z": lons // 2, "x_hi": 2, "x_lo": 2, "y": lats // 4, "core": 2}
    others = [name for name in sizes if name not in names]

    def places(wanted):
        return itertools.product(*[range(sizes[name]) for name in wanted])

    def device(at):
        lon = at["z"] * sizes["x_hi"] + at["x_hi"]
        lat = (at["x_lo"] * sizes["y"] + at["y"]) * sizes["core"] + at["core"]
        return lon * lats + lat

    return [
        [device(dict(zip(others, fixed)) | dict(zip(names, place))) for place in places(names)]
        for fixed in places(others)
    ]


def exchange(value, groups):
    return lax.all_to_all(value, ("lon", "lat"), 0, 0, axis_index_groups=groups)


def added(pieces):
    return jnp.sum(pieces.astype(F32), axis=0).astype(BF16)


def spread(piece, groups):
    return exchange(jnp.broadcast_to(piece[None], (len(groups[0]),) + piece.shape), groups)


def call(kernel, name, out_shape, scratch=(), in_specs=None, limit=16, micros=2):
    extra = {} if in_specs is None else {"in_specs": in_specs}
    return pl.pallas_call(
        kernel,
        out_shape=out_shape,
        scratch_shapes=list(scratch),
        compiler_params=pltpu.CompilerParams(vmem_limit_bytes=limit * 2**20),
        name=name,
        cost_estimate=pl.CostEstimate(
            flops=micros * 10**9, bytes_accessed=micros * 3 * 10**6, transcendentals=0
        ),
        **extra,
    )


def per_device(x_field, cotangent, gain, w_qkv, w_proj, bias_table, position_index, valid_rows):
    half_r, half_c = WH // 2, WW // 2
    x_own = x_field.transpose(1, 2, 0, 3)
    dy_own = cotangent.transpose(1, 2, 0, 3)

    def both(rows, cols):
        return jnp.concatenate([x_own[rows, cols], dy_own[rows, cols]], axis=3)

    top, bottom = slice(0, half_r), slice(half_r, WH)
    left, right = slice(0, half_c), slice(half_c, WW)
    east = shifted(both(bottom, left), -1, 0)
    corner = shifted(both(top, left), -1, -1)
    south = shifted(both(top, right), 0, -1)

    lat = lax.axis_index("lat").astype(jnp.int32)
    base = jnp.concatenate([jnp.stack([lat * WH, lat % 2]), valid_rows])
    vmem, smem = pl.BlockSpec(memory_space=pltpu.VMEM), pl.BlockSpec(memory_space=pltpu.SMEM)
    quarter = jax.ShapeDtypeStruct((half_r, half_c, Z, C), BF16)
    bias, inverse = call(
        bias_kernel,
        "bias_lookup",
        (
            jax.ShapeDtypeStruct((GROUPS, WIN, WIN), F32),
            jax.ShapeDtypeStruct((64, 128), jnp.int32),
        ),
        [
            pltpu.VMEM((GROUPS, CHUNKS * 128), F32),
            pltpu.VMEM((3, GROUPS * 24, 128), F32),
        ],
        [smem, vmem, vmem],
        micros=6,
    )(base, position_index, bias_table.transpose(1, 0, 2))

    half_w = jax.ShapeDtypeStruct((WROWS // 2, 128), BF16)
    back_own, back_east, back_south, back_corner, codes, kept, given = call(
        window_kernel,
        "window_grads",
        (
            quarter,
            quarter,
            quarter,
            quarter,
            jax.ShapeDtypeStruct((3, GROUPS * 24, 128), F32),
            half_w,
            half_w,
        ),
        [
            pltpu.VMEM((3, 576, 128), F32),
            pltpu.VMEM((3, 576, 128), F32),
            pltpu.VMEM((WROWS, 128), BF16),
        ],
        [smem] + [vmem] * 8,
        limit=24,
        micros=7,
    )(
        base,
        both(bottom, right),
        east,
        south,
        corner,
        bias,
        gain.reshape(1, C),
        w_qkv,
        w_proj,
    )

    taken = other_core(given)
    west = shifted(back_east, 1, 0)
    far = shifted(back_corner, 1, 1)
    north = shifted(back_south, 0, 1)
    packed = call(
        table_kernel,
        "table_grads",
        jax.ShapeDtypeStruct((TROWS, 128), BF16),
        [pltpu.VMEM((CHUNKS, GROUPS, 128), F32)],
    )(codes, inverse)

    lats, lons = lax.axis_size("lat"), lax.axis_size("lon")
    ring, cross = peers(("y", "z")), peers(("x_hi", "x_lo"))
    count = len(ring[0])
    w_rows, t_rows = WROWS // 2 // count, TROWS // count
    mine = (kept.astype(F32) + taken.astype(F32)).astype(BF16).reshape(count, w_rows, 128)
    sent = jnp.concatenate([mine, packed.reshape(count, t_rows, 128)], axis=1)
    parts = exchange(sent, ring)
    table_sums = added(parts[:, w_rows:].reshape(4, count // 4, t_rows, 128).swapaxes(0, 1))
    weight_sum = added(parts[:, :w_rows])
    table_sums = added(jnp.stack([table_sums, other_half(table_sums)]))
    weight_sum = added(spread(weight_sum, cross))
    both_sums = jnp.concatenate([jnp.stack([weight_sum] * 4), table_sums], axis=1)
    both_sums = jnp.broadcast_to(both_sums[:, None], (4, count // 4) + both_sums.shape[1:])
    got = exchange(both_sums.reshape(count, w_rows + t_rows, 128), ring)
    packed = got[:, w_rows:].reshape(TROWS, 128)
    kept = got[:, :w_rows].reshape(WROWS // 2, 128)
    taken = other_core(kept)

    upper = jnp.concatenate([far, north], axis=1)
    lower = jnp.concatenate([west, back_own], axis=1)
    back = jnp.concatenate([upper, lower], axis=0)
    d_field = (dy_own.astype(F32) + back.astype(F32)).astype(BF16).transpose(2, 0, 1, 3)

    tokens_total = Z * valid_rows.shape[0] * lons * WW
    d_gain, d_wqkv, d_wproj, d_table = call(
        functools.partial(finish_kernel, tokens_total**-0.5, (lons * WW) ** -0.5),
        "unpack",
        (
            jax.ShapeDtypeStruct((1, C), F32),
            jax.ShapeDtypeStruct((C, 3 * C), F32),
            jax.ShapeDtypeStruct((C, C), F32),
            jax.ShapeDtypeStruct((HEADS, TYPES, POS), F32),
        ),
        [pltpu.VMEM((WROWS, 128), BF16)],
        [smem] + [vmem] * 3,
    )(base, kept, taken, packed)
    return d_field, d_gain.reshape(C), d_wqkv, d_wproj, d_table.transpose(1, 0, 2)


def solution(mesh):
    field = P(None, "lat", "lon", None)
    table = P("lat", None, None)
    return jax.shard_map(
        per_device,
        mesh=mesh,
        in_specs=(field, field, P(), P(), P(), table, P(), P()),
        out_specs=(field, P(), P(), P(), table),
        check_vma=False,
    )
```
